512 devices in a mesh: chan: 16 (over z, core), exp: 32 (over x, y).
Axes of the slice: x: 4, y: 8, z: 8, core: 2. Of those that a mesh axis runs over, the one named last changes fastest.
Arguments:
- tokens: bfloat16 [96, 256, 2048], P('chan', 'exp'), may hold values from -6 to 6
- kernel: float32 [3, 3, 2048], replicated, may hold values from -2 to 2
- gain: float32 [2048], replicated, may hold values from 0.1 to 1.9
- routes: int32 [24576, 2], P(('chan', 'exp')), may hold values from 0 to 63, all different within a row; in each aligned block of 48 rows (0 to 47, 48 to 95, ...) at most 2 rows name the same one
- gate_num: int32 [24576, 2], P(('chan', 'exp')), may hold values from 1 to 15
- gate_proj: bfloat16 [512, 176, 2048], P(('exp', 'chan')), may hold values from -0.125 to 0.125
- up_proj: bfloat16 [512, 176, 2048], P(('exp', 'chan')), may hold values from -0.125 to 0.125
- down_proj: bfloat16 [512, 176, 2048], P(('exp', 'chan')), may hold values from -0.15625 to 0.15625
Outputs:
- mixed: bfloat16 [96, 256, 2048], P('chan', 'exp')
The draws below stay inside these ranges and needn't reach their ends.
Inputs may be any that keep to these rules, and one draw needn't show every extreme that they name: `routes`: the two ids of a row differ. Rows r * 48 to r * 48 + 47 are the tokens of one device, and in each such block no expert is named more than 2 times; some expert is named exactly 2 times in some blocks.
All inputs are finite; a program needn't handle non-finite values.
Results may differ from the reference program's by a relative error of at most 0.0085.
Values may be sent and summed in bfloat16 or wider, within the bound.
A program may use at most 64 MiB of HBM per device.

```python
import math
import jax
import jax.numpy as jnp
import numpy as np
from jax import lax

D = 2048
FF = 1408
EXPERTS = 64
SPLIT = 8
FFS = 176
CB = 6
TB = 8
TOK_DEV = 48
CAP = 2
NC = 96
NT = 256
TOKENS = 24576
N_CHAN = 16
N_EXP = 32


def with_ends(result, rng, low, largest):
    dims = result.shape
    place = [jax.random.randint(jax.random.fold_in(rng, axis), (), 0, dims[axis]) for axis in range(len(dims))]
    result = result.at[tuple(place)].set(low)
    longest = dims.index(max(dims))
    place[longest] = (place[longest] + 1) % dims[longest]
    return result.at[tuple(place)].set(largest)


def block_scale(own_key, extent, cuts, least, top_value):
    def one(dim, shards_of):
        steps = jax.random.uniform(jax.random.fold_in(jax.random.fold_in(own_key, 6), dim), (shards_of,), jnp.float32, least / len(cuts), top_value / len(cuts))
        return jnp.repeat(jnp.exp(steps), extent[dim] // shards_of).reshape((-1,) + (1,) * (len(extent) - dim - 1))

    level = one(*cuts[0])
    for cut in cuts[1:]:
        level = level * one(*cut)
    return level


def shared_out(own_key, own, number, rows, count, top, reach, skew):
    sequence = jax.random.permutation(own_key, count)
    heavy_load, usual = load_shares(count, rows * top, reach, skew, True), load_shares(count, rows * top, reach, skew, False)
    places = jnp.arange(count)

    def named(sizes, turn):
        used = int((sizes > 0).sum())
        fixed = max(1, used // 4)
        passed = fixed + (places - fixed + turn * (used - fixed)) % max(1, count - fixed)
        return jnp.zeros((count,), jnp.int32).at[sequence[jnp.where(places < fixed, places, passed)]].set(jnp.asarray(sizes, jnp.int32))

    sizes = jnp.where(number % 4 == 0, named(heavy_load, number // 4), named(usual, number - number // 4 - 1))
    mixed = jax.random.permutation(jax.random.fold_in(own, 3), count)
    donor, taker = mixed[0:count // 2 * 2:2], mixed[1:count // 2 * 2:2]
    slack = jnp.minimum(sizes[donor] - 1, reach - sizes[taker]) // 2
    slack = jnp.where((donor == sequence[0]) | (taker == sequence[0]) | (sizes[taker] == 0), 0, jnp.maximum(slack, 0))
    passed = jax.random.randint(jax.random.fold_in(own, 4), (count // 2,), 0, 1 << 20) % (slack + 1)
    sizes = sizes.at[donor].add(-passed).at[taker].add(passed)
    members = jnp.searchsorted(jnp.cumsum(sizes), jnp.arange(rows * top), side="right").astype(jnp.int32)
    table = members.reshape(top, rows).T
    table = table[jax.random.permutation(jax.random.fold_in(own, 1), rows)]
    turn = jax.random.randint(jax.random.fold_in(own, 2), (rows, 1), 0, top)
    return jnp.take_along_axis(table, (jnp.arange(top)[None, :] + turn) % top, axis=1)


def load_shares(count, total, limit, skew, full):
    loads = [(1 << 20) // math.isqrt(standing ** skew) + 1 for standing in range(1, count + 1)]
    largest = limit if full else min(limit, max(-(-total // count), total * loads[0] // sum(loads)))
    least = 1 if total - largest >= count - 1 else 0
    holding, surplus = [largest] + [least] * (count - 1), total - largest - least * (count - 1)
    while surplus > 0:
        candidates = [i for i in range(1, count) if holding[i] < largest] or [i for i in range(1, count) if holding[i] < limit]
        pool, budget = sum([loads[i] for i in candidates]), surplus
        for i in candidates:
            addition = min(limit - holding[i], max(1, budget * loads[i] // pool), surplus)
            holding[i] = holding[i] + addition
            surplus = surplus - addition
    return np.array(holding)


def gaussian(stream_key, dims, scale, reach, cuts=(), kind=jnp.bfloat16):
    factor_of = block_scale(stream_key, dims, cuts, -0.22, 0.18) if cuts else 1.0
    values = jax.random.normal(stream_key, dims, jnp.float32) * scale * factor_of
    return jnp.minimum(jnp.maximum(values, -reach), reach).astype(kind)


def setup_inputs(seed: int = 0) -> dict:
    key_of = jax.random.split(jax.random.key(seed), 9)
    tokens = gaussian(key_of[0], (NC, NT, D), 1.0, 6.0, ((0, 16), (1, 32)))
    kernel = gaussian(key_of[1], (3, 3, D), 9 ** -0.5, 2.0, (), jnp.float32)
    gain = jnp.clip(1.0 + 0.18 * jax.random.normal(key_of[2], (D,), jnp.float32), 0.1, 1.9)
    routes_keys = jax.random.split(jax.random.fold_in(key_of[3], 1), TOKENS // TOK_DEV)
    routes_turns = jax.random.permutation(jax.random.fold_in(key_of[3], 3), TOKENS // TOK_DEV)
    routes = jax.vmap(lambda own, number: shared_out(jax.random.fold_in(key_of[3], 2), own, number, TOK_DEV, EXPERTS, 2, CAP, 2))(routes_keys, routes_turns).reshape((TOKENS, 2))
    gate_num = with_ends(jax.random.randint(key_of[4], (TOKENS, 2), 1, 16), jax.random.fold_in(key_of[4], 1), 1, 15).astype(jnp.int32)
    gate_proj = gaussian(key_of[5], (EXPERTS * SPLIT, FFS, D), D ** -0.5, 0.125, ((0, 512),))
    up_proj = gaussian(key_of[6], (EXPERTS * SPLIT, FFS, D), D ** -0.5, 0.125, ((0, 512),))
    down_proj = gaussian(key_of[7], (EXPERTS * SPLIT, FFS, D), FF ** -0.5, 0.15625, ((0, 512),))
    return {"tokens": tokens, "kernel": kernel, "gain": gain, "routes": routes, "gate_num": gate_num, "gate_proj": gate_proj, "up_proj": up_proj, "down_proj": down_proj}


eps = 1e-06

def depthwise(padded, kernel, row_count, col_count):
    conv_sum = jnp.zeros((row_count, col_count, padded.shape[2]), jnp.float32)
    for row_shift in range(3):
        for col_shift in range(3):
            conv_sum = conv_sum + kernel[row_shift, col_shift] * padded[row_shift:row_shift + row_count, col_shift:col_shift + col_count]
    return conv_sum

def to_devices(grid_array):
    width = grid_array.shape[-1]
    moved = grid_array.reshape(N_CHAN, CB, N_EXP, TB, width).transpose(0, 2, 1, 3, 4)
    return moved.reshape(N_CHAN * N_EXP, TOK_DEV, width)

def reference(tokens, kernel, gain, routes, gate_num, gate_proj, up_proj, down_proj):
    device_count = N_CHAN * N_EXP
    padded = jnp.pad(tokens.astype(jnp.float32), ((1, 1), (1, 1), (0, 0)))
    conv_out = depthwise(padded, kernel, NC, NT)
    inverse_rms = lax.rsqrt(lax.optimization_barrier(jnp.mean(conv_out * conv_out, axis=2, keepdims=True)) + eps)
    normed = (conv_out * inverse_rms * gain).astype(jnp.bfloat16)
    ordered_conv = to_devices(conv_out)
    flat_norm = to_devices(normed).reshape(device_count * TOK_DEV, D)
    route_pairs = routes.reshape(device_count, 2 * TOK_DEV)
    onehot = (route_pairs[:, :, None] == jnp.arange(EXPERTS, dtype=jnp.int32)[None, None, :]).astype(jnp.int32)
    earlier = jnp.cumsum(onehot, axis=1) - onehot
    slot_rank = lax.optimization_barrier(jnp.sum(earlier * onehot, axis=2))
    device_ids = jnp.arange(device_count, dtype=jnp.int32)[:, None]
    position = ((route_pairs * device_count + device_ids) * CAP + slot_rank).astype(jnp.int32)
    source_token = (device_ids * TOK_DEV + jnp.arange(2 * TOK_DEV, dtype=jnp.int32)[None, :] // 2).astype(jnp.int32)
    slot_table = jnp.zeros((EXPERTS * device_count * CAP,), jnp.int32).at[position.reshape(-1)].set(source_token.reshape(-1))
    row_total = device_count * CAP

    def one_expert(expert_id):
        row_index = lax.dynamic_slice_in_dim(slot_table, expert_id * row_total, row_total, 0)
        row_block = flat_norm[row_index]
        gate_w = lax.dynamic_slice_in_dim(gate_proj, expert_id * SPLIT, SPLIT, 0).reshape(SPLIT * FFS, D)
        up_w = lax.dynamic_slice_in_dim(up_proj, expert_id * SPLIT, SPLIT, 0).reshape(SPLIT * FFS, D)
        down_w = lax.dynamic_slice_in_dim(down_proj, expert_id * SPLIT, SPLIT, 0)
        gate_val = lax.dot_general(row_block, gate_w, (((1,), (1,)), ((), ())), preferred_element_type=jnp.float32)
        up_val = lax.dot_general(row_block, up_w, (((1,), (1,)), ((), ())), preferred_element_type=jnp.float32)
        hidden = (jax.nn.silu(gate_val) * up_val).astype(jnp.bfloat16).reshape(row_total, SPLIT, FFS)
        down_part = jnp.einsum('rsf,sfd->srd', hidden.astype(jnp.float32), down_w.astype(jnp.float32), precision=lax.Precision.HIGHEST).astype(jnp.bfloat16)
        return lax.optimization_barrier(jnp.sum(down_part.astype(jnp.float32), axis=0)).astype(jnp.bfloat16)
    results = lax.map(one_expert, jnp.arange(EXPERTS, dtype=jnp.int32))
    picked = results.reshape(EXPERTS * row_total, D)[position.reshape(-1)]
    picked = picked.astype(jnp.float32).reshape(device_count, TOK_DEV, 2, D)
    numer = gate_num.astype(jnp.float32).reshape(device_count, TOK_DEV, 2)
    fraction = numer / lax.optimization_barrier(jnp.sum(numer, axis=2, keepdims=True))
    moe_out = lax.optimization_barrier(jnp.sum(picked * fraction[:, :, :, None], axis=2))
    mixed = (ordered_conv + moe_out).astype(jnp.bfloat16)
    mixed = mixed.reshape(N_CHAN, N_EXP, CB, TB, D).transpose(0, 2, 1, 3, 4)
    return mixed.reshape(NC, NT, D)
```

```python
import jax
import jax.numpy as jnp
from jax import lax
from jax.experimental import pallas as pl
from jax.experimental.pallas import tpu as pltpu
from jax.sharding import PartitionSpec as P

D = 2048
FFS = 176
CB = 6
TB = 8
TOK = CB * TB
NX, NY, NZ = 4, 8, 8
HALF = NZ // 2
CAP = 2
SLOTS = 2 * NX * NY * CAP
F = 4
FW = D // F
ROWS = NZ * NX * NY * CAP
EPS = 1e-06
MESH = pl.DeviceIdType.MESH
f32 = jnp.float32
bf16 = jnp.bfloat16


def iota(shape, dim):
    return lax.broadcasted_iota(jnp.int32, shape, dim)


def kernel(
    tok, taps, gain, routes, numer, wg, wu, wd, out,
    pg, pu, pd, row_send, row_halo, col_send, col_halo, img, conv,
    o_buf, a1, b1, a2, x_buf, y_buf, r_buf, s_buf, t_buf, u_buf, q_buf,
    w_send, w_recv, h_send, h_recv, send, recv,
):
    c = lax.axis_index("chan")
    e = lax.axis_index("exp")
    n_chan = 2 * NZ
    n_exp = NX * NY
    z, core = c // 2, c % 2
    x, y = e // NY, e % NY
    half = z // HALF

    def y_dev(k):
        return (c, x * NY + (y + k) % NY)

    def x_dev(k):
        return (c, ((x + k) % NX) * NY + y)

    def z_dev(k):
        return (((z + k) % NZ) * 2 + core, e)

    c_low, c_high = (c + n_chan - 1) % n_chan, (c + 1) % n_chan
    e_low, e_high = (e + n_exp - 1) % n_exp, (e + 1) % n_exp

    barrier = pltpu.get_barrier_semaphore()

    def greet(device):
        pl.semaphore_signal(barrier, inc=1, device_id=device, device_id_type=MESH)

    for device in ((c_low, e), (c_high, e), (c, e_low), (c, e_high)):
        greet(device)
    for count, device_of in ((NY, y_dev), (NX, x_dev), (NZ, z_dev)):
        lax.fori_loop(1, count, lambda k, _, d=device_of: (greet(d(k)), 0)[1], 0)

    row_send[0] = tok[0].astype(f32)
    row_send[1] = tok[CB - 1].astype(f32)
    pl.semaphore_wait(barrier, 4 + NY - 1 + NX - 1 + NZ - 1)

    def copy(src, dst, s, r, device):
        return pltpu.make_async_remote_copy(
            src_ref=src, dst_ref=dst, send_sem=s, recv_sem=r, device_id=device, device_id_type=MESH
        )

    row_copies = [
        copy(row_send.at[0], row_halo.at[1], h_send.at[0], h_recv.at[0], (c_low, e)),
        copy(row_send.at[1], row_halo.at[0], h_send.at[1], h_recv.at[1], (c_high, e)),
    ]
    for one in row_copies:
        one.start()
    partner = (z * 2 + 1 - core, e)
    weight_copies = [
        copy(src.at[0], dst, w_send.at[i], w_recv.at[i], partner)
        for i, (src, dst) in enumerate(((wg, pg), (wu, pu), (wd, pd)))
    ]

    for i in range(CB):
        img[i + 1] = tok[i].astype(f32)

    col = iota((TOK, SLOTS), 1)
    col_expert = 2 * ((col // 2 % NX) * NY + col // 16) + col // 8 % 2
    named = [(routes[:, q : q + 1] == col_expert).astype(f32) for q in range(2)]
    before = (iota((TOK, TOK), 0) > iota((TOK, TOK), 1)).astype(bf16)
    earlier = jnp.dot(before, (named[0] + named[1]).astype(bf16), preferred_element_type=f32)
    in_slot = (earlier == (col % 2).astype(f32)).astype(f32)
    number = numer[...].astype(f32)
    placing = (in_slot * (named[0] + named[1])).astype(bf16)
    weighting = (
        in_slot * (named[0] * number[:, 0:1] + named[1] * number[:, 1:2])
    ).astype(bf16)
    weight_sum = number[:, 0:1] + number[:, 1:2]

    to = iota((SLOTS, SLOTS), 0)
    frm = iota((SLOTS, SLOTS), 1)
    by_x = (
        (to % 16) // 2 * 16 + to // 16 % 2 * 8 + to // 32 * 2 + to % 2 == frm
    ).astype(bf16)
    by_y = (
        to // 2 % 4 * 32 + to // 8 % 2 * 16 + to // 16 * 2 + to % 2 == frm
    ).astype(bf16)

    for one in row_copies:
        one.wait()
    img[0] = jnp.where(c == 0, 0.0, row_halo[0])
    img[CB + 1] = jnp.where(c == n_chan - 1, 0.0, row_halo[1])
    for i in range(CB + 2):
        col_send[0, i : i + 1] = img[i, 0:1]
        col_send[1, i : i + 1] = img[i, TB - 1 : TB]
    col_copies = [
        copy(col_send.at[0], col_halo.at[1], h_send.at[2], h_recv.at[2], (c, e_low)),
        copy(col_send.at[1], col_halo.at[0], h_send.at[3], h_recv.at[3], (c, e_high)),
    ]
    for one in col_copies:
        one.start()
    for one in weight_copies:
        one.start()
    for one in col_copies:
        one.wait()

    first, last = e == 0, e == n_exp - 1
    squares = jnp.zeros((TOK, 1), f32)
    place = iota((TB, FW), 0)
    for f in range(F):
        cols = slice(f * FW, (f + 1) * FW)
        rows = []
        for i in range(CB + 2):
            middle = img[i, :, cols]
            low = jnp.where(first, 0.0, col_halo[0, i : i + 1, cols])
            high = jnp.where(last, 0.0, col_halo[1, i : i + 1, cols])
            rows.append((
                jnp.where(place == 0, low, pltpu.roll(middle, 1, 0)),
                middle,
                jnp.where(place == TB - 1, high, pltpu.roll(middle, TB - 1, 0)),
            ))
        for i in range(CB):
            total = jnp.zeros((TB, FW), f32)
            for a in range(3):
                for b in range(3):
                    total = total + taps[a, b : b + 1, cols] * rows[i + a][b]
            conv[i * TB : (i + 1) * TB, cols] = total
        block = conv[:, cols]
        squares = squares + jnp.sum(block * block, axis=1, keepdims=True)
    inverse = lax.rsqrt(squares * (1.0 / D) + EPS)

    def start(stage, f, count, src, dst, device_of):
        def one(k, _):
            copy(src(k), dst, send.at[stage, f], recv.at[stage, f], device_of(k)).start()
            return 0

        lax.fori_loop(1, count, one, 0)

    def wait_recv(stage, f, ref):
        pltpu.make_async_copy(ref, ref, recv.at[stage, f]).wait()

    def wait_send(stage, f, ref):
        pltpu.make_async_copy(ref, ref, send.at[stage, f]).wait()

    for f in range(F):
        cols = slice(f * FW, (f + 1) * FW)
        normed = (conv[:, cols] * inverse * gain[:, cols]).astype(bf16)
        o_buf[f] = lax.dot_general(
            placing, normed, (((0,), (0,)), ((), ())), preferred_element_type=f32
        ).astype(bf16).reshape(NY, 16, FW)
        start(0, f, NY, lambda k: o_buf.at[f, (y + k) % NY], a1.at[f, y], y_dev)
        a1[f, y] = o_buf[f, y]

    def to_z(f):
        wait_recv(1, f, a2.at[f, :, pl.ds(0, NX - 1)])
        start(2, f, NZ, lambda k: a2.at[f, (z + k) % NZ // HALF], x_buf.at[f, z], z_dev)
        x_buf[f, z] = a2[f, half]

    for f in range(F):
        wait_recv(0, f, a1.at[f, pl.ds(0, NY - 1)])
        b1[f] = jnp.dot(
            by_x, a1[f].reshape(SLOTS, FW), preferred_element_type=f32
        ).astype(bf16).reshape(NX, 2, 16, FW)
        start(1, f, NX, lambda k: b1.at[f, (x + k) % NX], a2.at[f, :, x], x_dev)
        a2[f, :, x] = b1[f, x]
        if f:
            to_z(f - 1)
    to_z(F - 1)

    for one in weight_copies:
        one.wait()
    totals = [jnp.zeros((ROWS, FFS), f32) for _ in range(4)]
    for f in range(F):
        cols = slice(f * FW, (f + 1) * FW)
        wait_recv(2, f, x_buf.at[f, pl.ds(0, NZ - 1)])
        block = x_buf[f].reshape(ROWS, FW)
        for i, w in enumerate((wg[0, :, cols], wu[0, :, cols], pg[:, cols], pu[:, cols])):
            totals[i] = totals[i] + lax.dot_general(
                block, w, (((1,), (1,)), ((), ())), preferred_element_type=f32
            )
    hidden = [
        (g / (1.0 + jnp.exp(-g)) * u).astype(bf16)
        for g, u in ((totals[0], totals[1]), (totals[2], totals[3]))
    ]

    for f in range(F):
        cols = slice(f * FW, (f + 1) * FW)
        part = jnp.dot(hidden[0], wd[0, :, cols], preferred_element_type=f32)
        part = part + jnp.dot(hidden[1], pd[:, cols], preferred_element_type=f32)
        y_buf[f] = part.astype(bf16).reshape(NZ, NX, 16, FW)
        start(3, f, NZ, lambda k: y_buf.at[f, (z + k) % NZ], r_buf.at[f, z], z_dev)
        r_buf[f, z] = y_buf[f, z]

    def back_y(f):
        wait_recv(4, f, t_buf.at[f, pl.ds(0, NX - 1)])
        u_buf[f] = jnp.dot(
            by_y, t_buf[f].reshape(SLOTS, FW), preferred_element_type=f32
        ).astype(bf16).reshape(NY, 16, FW)
        start(5, f, NY, lambda k: u_buf.at[f, (y + k) % NY], q_buf.at[f, y], y_dev)
        q_buf[f, y] = u_buf[f, y]

    def finish(f):
        cols = slice(f * FW, (f + 1) * FW)
        wait_recv(5, f, q_buf.at[f, pl.ds(0, NY - 1)])
        moe = jnp.dot(weighting, q_buf[f].reshape(SLOTS, FW), preferred_element_type=f32)
        mixed = conv[:, cols] + moe / weight_sum
        for i in range(CB):
            out[i, :, cols] = mixed[i * TB : (i + 1) * TB].astype(bf16)

    for f in range(F):
        wait_recv(3, f, r_buf.at[f, pl.ds(0, NZ - 1)])
        for h in range(2):
            total = r_buf[f, h * HALF].astype(f32)
            for k in range(1, HALF):
                total = total + r_buf[f, h * HALF + k].astype(f32)
            s_buf[f, h] = total.astype(bf16)
        start(4, f, NX, lambda k: s_buf.at[f, :, (x + k) % NX], t_buf.at[f, x], x_dev)
        t_buf[f, x] = s_buf[f, :, x]
        if f:
            back_y(f - 1)
        if f > 1:
            finish(f - 2)
    back_y(F - 1)
    finish(F - 2)
    finish(F - 1)

    for f in range(F):
        wait_send(0, f, o_buf.at[f, pl.ds(0, NY - 1)])
        wait_send(1, f, b1.at[f, pl.ds(0, NX - 1)])
        wait_send(2, f, x_buf.at[f, pl.ds(0, NZ - 1)])
        wait_send(3, f, y_buf.at[f, pl.ds(0, NZ - 1)])
        wait_send(4, f, t_buf.at[f, pl.ds(0, NX - 1)])
        wait_send(5, f, u_buf.at[f, pl.ds(0, NY - 1)])


def body(tokens, taps, gain, routes, gate_num, gate_proj, up_proj, down_proj):
    vmem = pl.BlockSpec(memory_space=pltpu.VMEM)
    dma = pltpu.SemaphoreType.DMA
    return pl.pallas_call(
        kernel,
        out_shape=jax.ShapeDtypeStruct((CB, TB, D), bf16),
        in_specs=[vmem] * 8,
        out_specs=vmem,
        scratch_shapes=[
            pltpu.VMEM((FFS, D), bf16),
            pltpu.VMEM((FFS, D), bf16),
            pltpu.VMEM((FFS, D), bf16),
            pltpu.VMEM((2, TB, D), f32),
            pltpu.VMEM((2, TB, D), f32),
            pltpu.VMEM((2, TB, D), f32),
            pltpu.VMEM((2, TB, D), f32),
            pltpu.VMEM((CB + 2, TB, D), f32),
            pltpu.VMEM((TOK, D), f32),
            pltpu.VMEM((F, NY, 16, FW), bf16),
            pltpu.VMEM((F, NY, 16, FW), bf16),
            pltpu.VMEM((F, NX, 2, 16, FW), bf16),
            pltpu.VMEM((F, 2, NX, 16, FW), bf16),
            pltpu.VMEM((F, NZ, NX, 16, FW), bf16),
            pltpu.VMEM((F, NZ, NX, 16, FW), bf16),
            pltpu.VMEM((F, NZ, NX, 16, FW), bf16),
            pltpu.VMEM((F, 2, NX, 16, FW), bf16),
            pltpu.VMEM((F, NX, 2, 16, FW), bf16),
            pltpu.VMEM((F, NY, 16, FW), bf16),
            pltpu.VMEM((F, NY, 16, FW), bf16),
            dma((3,)),
            dma((3,)),
            dma((4,)),
            dma((4,)),
            dma((6, F)),
            dma((6, F)),
        ],
        compiler_params=pltpu.CompilerParams(
            collective_id=0, has_side_effects=True, vmem_limit_bytes=48 * 2**20
        ),
    )(tokens, taps, gain.reshape(1, D), routes, gate_num, gate_proj, up_proj, down_proj)


def solution(mesh):
    return jax.shard_map(
        body,
        mesh=mesh,
        in_specs=(
            P("chan", "exp", None),
            P(),
            P(),
            P(("chan", "exp"), None),
            P(("chan", "exp"), None),
            P(("exp", "chan"), None, None),
            P(("exp", "chan"), None, None),
            P(("exp", "chan"), None, None),
        ),
        out_specs=P("chan", "exp", None),
        check_vma=False,
    )
```

```python
import jax
import jax.numpy as jnp
from jax import lax
from jax.experimental import pallas as pl
from jax.experimental.pallas import tpu as pltpu
from jax.sharding import PartitionSpec as P

D = 2048
FFS = 176
CB = 6
TB = 8
TOK = CB * TB
NX, NY, NZ = 4, 8, 8
HALF = NZ // 2
CAP = 2
SLOTS = 2 * NX * NY * CAP
BLOCK = NX * NY * CAP
F = 4
FW = D // F
FH = FW // 2
FAR = 5
EPS = 1e-06
MESH = pl.DeviceIdType.MESH
f32 = jnp.float32
bf16 = jnp.bfloat16


def iota(shape, dim):
    return lax.broadcasted_iota(jnp.int32, shape, dim)


def loop(low, high, step):
    def one(k, carry):
        step(k)
        return carry

    lax.fori_loop(low, high, one, 0)


def kernel(
    tok_in, taps_in, gain_in, routes_in, numer_in, wg_in, wu_in, wd_in, out,
    tok, taps, gain, routes, numer, wg, wu, wd,
    pg, pu, pd, row_send, row_halo, col_send, col_halo, img, conv,
    o_buf, a1, b1, a2, x_buf, p_buf, r_buf, s_buf, t_buf, u_buf, q_buf,
    in_sem, w_send, w_recv, h_send, h_recv, y_send, y_recv, x_send, x_recv,
    go_send, go_recv, back_send, back_recv, xb_send, xb_recv, yb_send, yb_recv,
):
    c = lax.axis_index("chan")
    e = lax.axis_index("exp")
    n_chan = 2 * NZ
    n_exp = NX * NY
    z, core = c // 2, c % 2
    x, y = e // NY, e % NY
    half = z // HALF

    local = [
        pltpu.make_async_copy(src, dst, in_sem.at[i])
        for i, (src, dst) in enumerate((
            (tok_in, tok), (taps_in, taps), (routes_in, routes), (numer_in, numer),
            (gain_in, gain), (wg_in, wg), (wu_in, wu), (wd_in, wd),
        ))
    ]
    for one in local:
        one.start()

    def y_dev(k):
        return (c, x * NY + (y + k) % NY)

    def x_dev(k):
        return (c, ((x + k) % NX) * NY + y)

    def z_dev(k):
        return (((z + k + NZ) % NZ) * 2 + core, e)

    c_low, c_high = (c + n_chan - 1) % n_chan, (c + 1) % n_chan
    e_low, e_high = (e + n_exp - 1) % n_exp, (e + 1) % n_exp

    barrier = pltpu.get_barrier_semaphore()

    def greet(device):
        pl.semaphore_signal(barrier, inc=1, device_id=device, device_id_type=MESH)

    for device in (
        (c_low, e), (c_high, e), (c, e_low), (c, e_high), z_dev(1), z_dev(-1)
    ):
        greet(device)
    loop(1, NY, lambda k: greet(y_dev(k)))
    loop(1, NX, lambda k: greet(x_dev(k)))

    local[0].wait()
    row_send[0] = tok[0].astype(f32)
    row_send[1] = tok[CB - 1].astype(f32)
    for i in range(CB):
        img[i + 1] = tok[i].astype(f32)
    for one in local[1:5]:
        one.wait()

    before = (iota((TOK, TOK), 0) < iota((TOK, TOK), 1)).astype(bf16)

    def chosen(expert, cap):
        named = [(routes[q : q + 1] == expert).astype(f32) for q in range(2)]
        earlier = jnp.dot(
            (named[0] + named[1]).astype(bf16), before, preferred_element_type=f32
        )
        in_slot = (earlier == cap.astype(f32)).astype(f32)
        return in_slot * named[0], in_slot * named[1]

    slot = iota((SLOTS, TOK), 0)
    first, second = chosen(
        2 * ((slot // 2 % NX) * NY + slot // 16) + slot // 8 % 2, slot % 2
    )
    placing = (first + second).astype(bf16)
    number = numer[...].astype(f32)
    weighting = []
    for h in (half, 1 - half):
        first, second = chosen(2 * ((slot // 2 % NX) * NY + slot // 16) + h, slot % 2)
        both = first * number[0:1] + second * number[1:2]
        weighting.append([
            (both * (slot // 8 % 2 == part).astype(f32)).astype(bf16) for part in range(2)
        ])
    square = iota((TOK, TOK), 0) == iota((TOK, TOK), 1)
    weight_sum = jnp.sum(
        jnp.where(square, number[0:1] + number[1:2], 0.0), axis=1, keepdims=True
    )

    to = iota((SLOTS, SLOTS), 0)
    by_x = (
        to % 16 // 2 * 16 + to // 16 % 2 * 8 + to // 32 * 2 + to % 2 == iota((SLOTS, SLOTS), 1)
    ).astype(bf16)
    to = iota((SLOTS, BLOCK), 0)
    found = to // 2 % NX * 16 + to // 16 * 2 + to % 2 == iota((SLOTS, BLOCK), 1)
    by_y = [(found & (to // 8 % 2 == part)).astype(bf16) for part in range(2)]

    pl.semaphore_wait(barrier, 6 + NY - 1 + NX - 1)

    def copy(src, dst, s, r, device):
        return pltpu.make_async_remote_copy(
            src_ref=src, dst_ref=dst, send_sem=s, recv_sem=r, device_id=device, device_id_type=MESH
        )

    row_copies = [
        copy(row_send.at[0], row_halo.at[1], h_send.at[0], h_recv.at[0], (c_low, e)),
        copy(row_send.at[1], row_halo.at[0], h_send.at[1], h_recv.at[1], (c_high, e)),
    ]
    for one in row_copies:
        one.start()
    partner = (z * 2 + 1 - core, e)
    for one in local[5:]:
        one.wait()
    weight_copies = [
        copy(src.at[0], dst, w_send.at[i], w_recv.at[i], partner)
        for i, (src, dst) in enumerate(((wg, pg), (wu, pu), (wd, pd)))
    ]

    for one in row_copies:
        one.wait()
    img[0] = jnp.where(c == 0, 0.0, row_halo[0])
    img[CB + 1] = jnp.where(c == n_chan - 1, 0.0, row_halo[1])
    for i in range(CB + 2):
        col_send[0, i : i + 1] = img[i, 0:1]
        col_send[1, i : i + 1] = img[i, TB - 1 : TB]
    col_copies = [
        copy(col_send.at[0], col_halo.at[1], h_send.at[2], h_recv.at[2], (c, e_low)),
        copy(col_send.at[1], col_halo.at[0], h_send.at[3], h_recv.at[3], (c, e_high)),
    ]
    for one in col_copies:
        one.start()
    for one in weight_copies:
        one.start()
    for one in col_copies:
        one.wait()

    left_end, right_end = e == 0, e == n_exp - 1
    squares = jnp.zeros((TOK, 1), f32)
    place = iota((TB, FW), 0)
    for f in range(F):
        cols = slice(f * FW, (f + 1) * FW)
        rows = []
        for i in range(CB + 2):
            middle = img[i, :, cols]
            low = jnp.where(left_end, 0.0, col_halo[0, i : i + 1, cols])
            high = jnp.where(right_end, 0.0, col_halo[1, i : i + 1, cols])
            rows.append((
                jnp.where(place == 0, low, pltpu.roll(middle, 1, 0)),
                middle,
                jnp.where(place == TB - 1, high, pltpu.roll(middle, TB - 1, 0)),
            ))
        for i in range(CB):
            total = jnp.zeros((TB, FW), f32)
            for a in range(3):
                for b in range(3):
                    total = total + taps[a, b : b + 1, cols] * rows[i + a][b]
            conv[i * TB : (i + 1) * TB, cols] = total
        block = conv[:, cols]
        squares = squares + jnp.sum(block * block, axis=1, keepdims=True)
    inverse = lax.rsqrt(squares * (1.0 / D) + EPS)

    def wait_all(ref, sem):
        pltpu.make_async_copy(ref, ref, sem).wait()

    for f in range(F):
        cols = slice(f * FW, (f + 1) * FW)
        normed = (conv[:, cols] * inverse * gain[:, cols]).astype(bf16)
        o_buf[f] = jnp.dot(placing, normed, preferred_element_type=f32).astype(
            bf16
        ).reshape(NY, 16, FW)
        loop(1, NY, lambda k: copy(
            o_buf.at[f, (y + k) % NY], a1.at[f, y], y_send.at[f], y_recv.at[f], y_dev(k)
        ).start())
        a1[f, y] = o_buf[f, y]

    def chain(way):
        h, up = way // 2, way % 2
        u = (z + NZ - HALF * h) % NZ
        at = ((1 - 2 * up) * u + 3 * up + NZ) % NZ
        return h, up, at

    def source(h, up, s):
        return ((1 - 2 * up) * s + 3 * up + HALF * h + NZ) % NZ

    def go(h, up, s, f, src):
        way, zs = 2 * h + up, source(h, up, s)
        return copy(
            src, x_buf.at[h, zs, f], go_send.at[way, s - 1, f], go_recv.at[way, s - 1, f],
            z_dev(2 * up - 1),
        )

    def back(h, up, s, f, src):
        way, zs = 2 * h + up, source(h, up, s)
        return copy(
            src, r_buf.at[h, up, zs, f], back_send.at[way, s - 1, f], back_recv.at[way, s - 1, f],
            z_dev(1 - 2 * up),
        )

    def send_own(f):
        def step(way):
            h, up, at = chain(way)

            @pl.when((at >= 1) & (at <= FAR))
            def _():
                go(h, up, at, f, a2.at[f, h]).start()

        loop(0, 4, step)

    def pass_on(t):
        def step(i):
            f, way = i // 4, i % 4
            h, up, at = chain(way)
            s = at + t

            @pl.when(s <= FAR)
            def _():
                block = x_buf.at[h, source(h, up, s), f]
                go(h, up, s, f, block).wait_recv()

                @pl.when(at >= 1)
                def _():
                    go(h, up, s, f, block).start()

        loop(0, 4 * F, step)

    def first_back(s):
        def step(i):
            f, way = i // 4, i % 4
            h, up, at = chain(way)

            @pl.when(at == 0)
            def _():
                back(h, up, s, f, p_buf.at[source(h, up, s), f]).start()

        loop(0, 4 * F, step)

    def next_back(t):
        def step(i):
            f, way = i // 4, i % 4
            h, up, at = chain(way)
            s = t - at

            @pl.when((at >= 1) & (at <= s) & (s <= FAR))
            def _():
                zs = source(h, up, s)
                back(h, up, s, f, r_buf.at[h, up, zs, f]).wait_recv()

                @pl.when((at < HALF) & (at < s))
                def _():
                    r_buf[h, up, zs, f] = (
                        r_buf[h, up, zs, f].astype(f32) + p_buf[zs, f].astype(f32)
                    ).astype(bf16)

                @pl.when(at < s)
                def _():
                    back(h, up, s, f, r_buf.at[h, up, zs, f]).start()

        loop(0, 4 * F, step)

    def experts(blocks):
        size = BLOCK * len(blocks)
        totals = [jnp.zeros((size, FFS), f32) for _ in range(4)]
        for f in range(F):
            cols = slice(f * FW, (f + 1) * FW)
            rows = [x_buf[half, zs, f].reshape(BLOCK, FW) for zs in blocks]
            rows = rows[0] if len(rows) == 1 else jnp.concatenate(rows, axis=0)
            for i, w in enumerate((wg[0, :, cols], wu[0, :, cols], pg[:, cols], pu[:, cols])):
                totals[i] = totals[i] + lax.dot_general(
                    rows, w, (((1,), (1,)), ((), ())), preferred_element_type=f32
                )
        hidden = [
            (g / (1.0 + jnp.exp(-g)) * u).astype(bf16)
            for g, u in ((totals[0], totals[1]), (totals[2], totals[3]))
        ]
        for f in range(F):
            cols = slice(f * FW, (f + 1) * FW)
            part = jnp.dot(hidden[0], wd[0, :, cols], preferred_element_type=f32)
            part = part + jnp.dot(hidden[1], pd[:, cols], preferred_element_type=f32)
            for i, zs in enumerate(blocks):
                p_buf[zs, f] = part[i * BLOCK : (i + 1) * BLOCK].astype(bf16).reshape(
                    NX, 16, FW
                )

    def gathered(f):
        wait_all(a2.at[f, :, pl.ds(0, NX - 1)], x_recv.at[f])
        send_own(f)
        x_buf[half, z, f] = a2[f, half]

    for f in range(F):
        wait_all(a1.at[f, pl.ds(0, NY - 1)], y_recv.at[f])
        b1[f] = jnp.dot(
            by_x, a1[f].reshape(SLOTS, FW), preferred_element_type=f32
        ).astype(bf16).reshape(NX, 2, 16, FW)
        loop(1, NX, lambda k: copy(
            b1.at[f, (x + k) % NX], a2.at[f, :, x], x_send.at[f], x_recv.at[f], x_dev(k)
        ).start())
        a2[f, :, x] = b1[f, x]
        if f:
            gathered(f - 1)
    gathered(F - 1)
    for one in weight_copies:
        one.wait()

    def back_x(o):
        h = half if o == 0 else 1 - half
        for f in range(F):
            total = jnp.zeros((NX, 16, FW), f32)
            if o == 0:
                total = p_buf[z, f].astype(f32)
            for up in range(2):
                at = chain(2 * h + up)[2]
                there = (at >= 1) & (at <= FAR)
                total = total + jnp.where(there, r_buf[h, up, z, f].astype(f32), 0.0)
            s_buf[o, f] = total.astype(bf16)
            loop(1, NX, lambda k: copy(
                s_buf.at[o, f, (x + k) % NX], t_buf.at[o, f, x],
                xb_send.at[o, f], xb_recv.at[o, f], x_dev(k),
            ).start())
            t_buf[o, f, x] = s_buf[o, f, x]

    def back_y(o):
        for f in range(F):
            wait_all(t_buf.at[o, f, pl.ds(0, NX - 1)], xb_recv.at[o, f])
            rows = t_buf[o, f].reshape(BLOCK, FW)
            total = jnp.dot(by_y[0], rows[:, :FH], preferred_element_type=f32)
            total = total + jnp.dot(by_y[1], rows[:, FH:], preferred_element_type=f32)
            u_buf[o, f] = total.astype(bf16).reshape(NY, 16, FH)
            loop(1, NY, lambda k: copy(
                u_buf.at[o, f, (y + k) % NY], q_buf.at[o, f, y],
                yb_send.at[o, f], yb_recv.at[o, f], y_dev(k),
            ).start())
            q_buf[o, f, y] = u_buf[o, f, y]

    u = z % HALF
    near = u // 2

    def at_distance(up, t):
        at = u if up == 0 else 3 - u
        return source(half, up, at + t)

    def at_far(up, t):
        return source(half, up, (1 - 2 * up) * u + 3 * up + t)

    experts([z])
    for t in range(1, 2 * FAR + 1):
        if t <= FAR:
            pass_on(t)
            if t <= 2:
                experts([at_distance(0, t), at_distance(1, t)])
            elif t <= 4:
                experts([at_far(near, t)])
            if t == 3:

                @pl.when((u == 1) | (u == 2))
                def _():
                    experts([at_far(1 - near, 3)])

            if t == 5:

                @pl.when((u == 0) | (u == 3))
                def _():
                    experts([at_far(near, 5)])

            first_back(t)
        if t > 1:
            next_back(t)
        if t == 6:
            back_x(0)
        if t == 7:
            back_y(0)
    back_x(1)

    def sent(i):
        f, s, way = i % F, i // F % FAR + 1, i // (F * FAR)
        h, up, at = chain(way)

        @pl.when((at >= 1) & (at <= s))
        def _():
            go(h, up, s, f, a2.at[f, h]).wait_send()

        @pl.when(at < s)
        def _():
            back(h, up, s, f, p_buf.at[0, f]).wait_send()

    loop(0, 4 * FAR * F, sent)
    back_y(1)
    for f in range(F):
        wait_all(o_buf.at[f, pl.ds(0, NY - 1)], y_send.at[f])
        wait_all(a2.at[f, :, pl.ds(0, NX - 1)], x_send.at[f])
        for o in range(2):
            wait_all(t_buf.at[o, f, pl.ds(0, NX - 1)], xb_send.at[o, f])
        wait_all(q_buf.at[0, f, pl.ds(0, NY - 1)], yb_recv.at[0, f])
        wait_all(q_buf.at[1, f, pl.ds(0, NY - 1)], yb_recv.at[1, f])
        for part in range(2):
            cols = slice(f * FW + part * FH, f * FW + (part + 1) * FH)
            moe = jnp.zeros((TOK, FH), f32)
            for o in range(2):
                moe = moe + lax.dot_general(
                    weighting[o][part], q_buf[o, f].reshape(SLOTS, FH),
                    (((0,), (0,)), ((), ())), preferred_element_type=f32,
                )
            mixed = conv[:, cols] + moe / weight_sum
            for i in range(CB):
                out[i, :, cols] = mixed[i * TB : (i + 1) * TB].astype(bf16)
    for f in range(F):
        for o in range(2):
            wait_all(u_buf.at[o, f, pl.ds(0, NY - 1)], yb_send.at[o, f])


def body(tokens, taps, gain, routes, gate_num, gate_proj, up_proj, down_proj):
    anywhere = pl.BlockSpec(memory_space=pl.ANY)
    vmem = pltpu.VMEM
    dma = pltpu.SemaphoreType.DMA
    return pl.pallas_call(
        kernel,
        out_shape=jax.ShapeDtypeStruct((CB, TB, D), bf16),
        in_specs=[anywhere] * 8,
        out_specs=pl.BlockSpec(memory_space=pltpu.VMEM),
        scratch_shapes=[
            vmem((CB, TB, D), bf16),
            vmem((3, 3, D), f32),
            vmem((1, D), f32),
            vmem((2, TOK), jnp.int32),
            vmem((2, TOK), jnp.int32),
            vmem((1, FFS, D), bf16),
            vmem((1, FFS, D), bf16),
            vmem((1, FFS, D), bf16),
            vmem((FFS, D), bf16),
            vmem((FFS, D), bf16),
            vmem((FFS, D), bf16),
            vmem((2, TB, D), f32),
            vmem((2, TB, D), f32),
            vmem((2, TB, D), f32),
            vmem((2, TB, D), f32),
            vmem((CB + 2, TB, D), f32),
            vmem((TOK, D), f32),
            vmem((F, NY, 16, FW), bf16),
            vmem((F, NY, 16, FW), bf16),
            vmem((F, NX, 2, 16, FW), bf16),
            vmem((F, 2, NX, 16, FW), bf16),
            vmem((2, NZ, F, NX, 16, FW), bf16),
            vmem((NZ, F, NX, 16, FW), bf16),
            vmem((2, 2, NZ, F, NX, 16, FW), bf16),
            vmem((2, F, NX, 16, FW), bf16),
            vmem((2, F, NX, 16, FW), bf16),
            vmem((2, F, NY, 16, FH), bf16),
            vmem((2, F, NY, 16, FH), bf16),
            dma((8,)),
            dma((3,)),
            dma((3,)),
            dma((4,)),
            dma((4,)),
            dma((F,)),
            dma((F,)),
            dma((F,)),
            dma((F,)),
            dma((4, FAR, F)),
            dma((4, FAR, F)),
            dma((4, FAR, F)),
            dma((4, FAR, F)),
            dma((2, F)),
            dma((2, F)),
            dma((2, F)),
            dma((2, F)),
        ],
        compiler_params=pltpu.CompilerParams(
            collective_id=0, has_side_effects=True, vmem_limit_bytes=56 * 2**20
        ),
    )(
        tokens, taps, gain.reshape(1, D), routes.T, gate_num.T, gate_proj, up_proj, down_proj
    )


def solution(mesh):
    return jax.shard_map(
        body,
        mesh=mesh,
        in_specs=(
            P("chan", "exp", None),
            P(),
            P(),
            P(("chan", "exp"), None),
            P(("chan", "exp"), None),
            P(("exp", "chan"), None, None),
            P(("exp", "chan"), None, None),
            P(("exp", "chan"), None, None),
        ),
        out_specs=P("chan", "exp", None),
        check_vma=False,
    )
```

```python
import jax
import jax.numpy as jnp
from jax import lax
from jax.experimental import pallas as pl
from jax.experimental.pallas import tpu as pltpu
from jax.sharding import PartitionSpec as P

D = 2048
FFS = 176
CB = 6
TB = 8
TOK = CB * TB
NX, NY, NZ = 4, 8, 8
HALF = NZ // 2
CAP = 2
SLOTS = 2 * NX * NY * CAP
BLOCK = NX * NY * CAP
F = 4
FW = D // F
FH = FW // 2
FAR = 5
EPS = 1e-06
MESH = pl.DeviceIdType.MESH
f32 = jnp.float32
bf16 = jnp.bfloat16


def iota(shape, dim):
    return lax.broadcasted_iota(jnp.int32, shape, dim)


def loop(low, high, step):
    def one(k, carry):
        step(k)
        return carry

    lax.fori_loop(low, high, one, 0)


def kernel(
    tok_in, taps_in, gain_in, routes_in, numer_in, wg_in, wu_in, wd_in, out,
    tok, taps, gain, routes, numer, w_in, w_out,
    row_send, row_halo, col_send, col_halo, end_send, end_halo, img, conv,
    o_buf, a1, b1, a2, x_buf, p_buf, r_buf, s_buf, t_buf, u_buf, q_buf,
    in_sem, w_send, w_recv, h_send, h_recv, y_send, y_recv, x_send, x_recv,
    go_send, go_recv, back_send, back_recv, xb_send, xb_recv, yb_send, yb_recv,
):
    c = lax.axis_index("chan")
    e = lax.axis_index("exp")
    n_chan = 2 * NZ
    n_exp = NX * NY
    z, core = c // 2, c % 2
    x, y = e // NY, e % NY
    half = z // HALF

    def y_dev(k):
        return (c, x * NY + (y + k) % NY)

    def x_dev(k):
        return (c, ((x + k) % NX) * NY + y)

    def z_dev(k):
        return (((z + k + NZ) % NZ) * 2 + core, e)

    c_low, c_high = (c + n_chan - 1) % n_chan, (c + 1) % n_chan
    e_low, e_high = (e + n_exp - 1) % n_exp, (e + 1) % n_exp

    barrier = pltpu.get_barrier_semaphore()

    def greet(device):
        pl.semaphore_signal(barrier, inc=1, device_id=device, device_id_type=MESH)

    for device in (
        (c_low, e), (c_high, e), (c, e_low), (c, e_high),
        z_dev(1), z_dev(-1), z_dev(2), z_dev(-2),
        (c_low, e_low), (c_low, e_high), (c_high, e_low), (c_high, e_high),
    ):
        greet(device)
    loop(1, NY, lambda k: greet(y_dev(k)))
    loop(1, NX, lambda k: greet(x_dev(k)))

    local = [
        pltpu.make_async_copy(src, dst, in_sem.at[i])
        for i, (src, dst) in enumerate((
            (tok_in, tok), (taps_in, taps), (routes_in, routes), (numer_in, numer),
            (gain_in, gain), (wg_in.at[0], w_in.at[0, 0]), (wu_in.at[0], w_in.at[1, 0]),
            (wd_in.at[0], w_out.at[0]),
        ))
    ]
    for one in local:
        one.start()

    for side in range(2):
        for i in (0, CB + 1):
            col_send[side, i : i + 1] = jnp.zeros((1, D), f32)
    local[0].wait()
    for i in range(CB):
        block = tok[i].astype(f32)
        img[i + 1] = block
        for side, j in enumerate((0, TB - 1)):
            col_send[side, i + 1 : i + 2] = block[j : j + 1]
        for end in range(2):
            if i == end * (CB - 1):
                row_send[end] = block
                for side, j in enumerate((0, TB - 1)):
                    end_send[end, side] = block[j : j + 1]
    pl.semaphore_wait(barrier, 12 + NY - 1 + NX - 1)

    def copy(src, dst, s, r, device):
        return pltpu.make_async_remote_copy(
            src_ref=src, dst_ref=dst, send_sem=s, recv_sem=r, device_id=device, device_id_type=MESH
        )

    c_ends, e_ends = (c_low, c_high), (e_low, e_high)
    halo_copies = []
    for end in range(2):
        for side in range(2):
            i = 4 + 2 * end + side
            halo_copies.append(copy(
                end_send.at[end, side], end_halo.at[1 - end, 1 - side],
                h_send.at[i], h_recv.at[i], (c_ends[end], e_ends[side]),
            ))
    for end in range(2):
        halo_copies.append(copy(
            row_send.at[end], row_halo.at[1 - end], h_send.at[end], h_recv.at[end],
            (c_ends[end], e),
        ))
        halo_copies.append(copy(
            col_send.at[end], col_halo.at[1 - end], h_send.at[2 + end], h_recv.at[2 + end],
            (c, e_ends[end]),
        ))
    for one in halo_copies:
        one.start()
    partner = (z * 2 + 1 - core, e)
    for one in local[5:]:
        one.wait()
    weight_copies = [
        copy(src, dst, w_send.at[i], w_recv.at[i], partner)
        for i, (src, dst) in enumerate((
            (w_in.at[0, 0], w_in.at[0, 1]), (w_in.at[1, 0], w_in.at[1, 1]),
            (w_out.at[0], w_out.at[1]),
        ))
    ]

    for one in local[1:5]:
        one.wait()

    before = (iota((TOK, TOK), 0) < iota((TOK, TOK), 1)).astype(bf16)

    def chosen(expert, cap):
        named = [(routes[q : q + 1] == expert).astype(f32) for q in range(2)]
        earlier = jnp.dot(
            (named[0] + named[1]).astype(bf16), before, preferred_element_type=f32
        )
        in_slot = (earlier == cap.astype(f32)).astype(f32)
        return in_slot * named[0], in_slot * named[1]

    slot = iota((SLOTS, TOK), 0)
    first, second = chosen(
        2 * ((slot // 2 % NX) * NY + slot // 16) + slot // 8 % 2, slot % 2
    )
    placing = (first + second).astype(bf16)
    number = numer[...].astype(f32)
    weighting = []
    for h in (half, 1 - half):
        first, second = chosen(2 * ((slot // 2 % NX) * NY + slot // 16) + h, slot % 2)
        both = first * number[0:1] + second * number[1:2]
        weighting.append([
            (both * (slot // 8 % 2 == part).astype(f32)).astype(bf16) for part in range(2)
        ])
    square = iota((TOK, TOK), 0) == iota((TOK, TOK), 1)
    weight_sum = jnp.sum(
        jnp.where(square, number[0:1] + number[1:2], 0.0), axis=1, keepdims=True
    )

    to = iota((SLOTS, SLOTS), 0)
    by_x = (
        to % 16 // 2 * 16 + to // 16 % 2 * 8 + to // 32 * 2 + to % 2 == iota((SLOTS, SLOTS), 1)
    ).astype(bf16)
    to = iota((SLOTS, BLOCK), 0)
    found = to // 2 % NX * 16 + to // 16 * 2 + to % 2 == iota((SLOTS, BLOCK), 1)
    by_y = [(found & (to // 8 % 2 == part)).astype(bf16) for part in range(2)]

    for one in weight_copies:
        one.start()
    for one in halo_copies:
        one.wait()
    img[0] = jnp.where(c == 0, 0.0, row_halo[0])
    img[CB + 1] = jnp.where(c == n_chan - 1, 0.0, row_halo[1])
    for side in range(2):
        col_halo[side, 0:1] = jnp.where(c == 0, 0.0, end_halo[0, side])
        col_halo[side, CB + 1 : CB + 2] = jnp.where(c == n_chan - 1, 0.0, end_halo[1, side])

    left_end, right_end = e == 0, e == n_exp - 1
    squares = jnp.zeros((TOK, 1), f32)
    place = iota((TB, FW), 0)
    for f in range(F):
        cols = slice(f * FW, (f + 1) * FW)
        rows = []
        for i in range(CB + 2):
            middle = img[i, :, cols]
            low = jnp.where(left_end, 0.0, col_halo[0, i : i + 1, cols])
            high = jnp.where(right_end, 0.0, col_halo[1, i : i + 1, cols])
            rows.append((
                jnp.where(place == 0, low, pltpu.roll(middle, 1, 0)),
                middle,
                jnp.where(place == TB - 1, high, pltpu.roll(middle, TB - 1, 0)),
            ))
        for i in range(CB):
            total = jnp.zeros((TB, FW), f32)
            for a in range(3):
                for b in range(3):
                    total = total + taps[a, b : b + 1, cols] * rows[i + a][b]
            conv[i * TB : (i + 1) * TB, cols] = total
        block = conv[:, cols]
        squares = squares + jnp.sum(block * block, axis=1, keepdims=True)
    inverse = lax.rsqrt(squares * (1.0 / D) + EPS)

    def wait_all(ref, sem):
        pltpu.make_async_copy(ref, ref, sem).wait()

    for f in range(F):
        cols = slice(f * FW, (f + 1) * FW)
        normed = (conv[:, cols] * inverse * gain[:, cols]).astype(bf16)
        o_buf[f] = jnp.dot(placing, normed, preferred_element_type=f32).astype(
            bf16
        ).reshape(NY, 16, FW)
        loop(1, NY, lambda k: copy(
            o_buf.at[f, (y + k) % NY], a1.at[f, y], y_send.at[f], y_recv.at[f], y_dev(k)
        ).start())
        a1[f, y] = o_buf[f, y]

    u = z % HALF
    places = (u, HALF - 1 - u)
    near = u // 2
    far = HALF + u + near * (HALF - 1 - 2 * u)

    def source(h, up, s):
        return ((1 - 2 * up) * s + 3 * up + HALF * h + NZ) % NZ

    def go(h, up, s, f, src, hop=1):
        way, zs = 2 * h + up, source(h, up, s)
        return copy(
            src, x_buf.at[h, zs, f], go_send.at[way, s - 1, f], go_recv.at[way, s - 1, f],
            z_dev((2 * up - 1) * hop),
        )

    def back(h, up, s, f, src, hop=1):
        way, zs = 2 * h + up, source(h, up, s)
        return copy(
            src, r_buf.at[h, up, zs, f], back_send.at[way, s - 1, f], back_recv.at[way, s - 1, f],
            z_dev((1 - 2 * up) * hop),
        )

    def send_own(f):
        go(1 - half, near, far, f, a2.at[f, 1 - half], far - HALF + 1).start()
        for up, at in enumerate(places):

            @pl.when(at >= 1)
            def _():
                go(half, up, at, f, a2.at[f, half]).start()

    def pass_on(t):
        def step(f):
            for up, at in enumerate(places):
                s = at + t

                @pl.when(s <= FAR)
                def _():
                    block = x_buf.at[half, source(half, up, s), f]
                    go(half, up, s, f, block).wait_recv()

                    @pl.when(at >= 1)
                    def _():
                        go(half, up, s, f, block).start()

        loop(0, F, step)

    def first_back(s):
        for up, at in enumerate(places):

            @pl.when(at == 0)
            def _():
                zs = source(half, up, s)
                loop(0, F, lambda f: back(half, up, s, f, p_buf.at[zs, f]).start())

    def next_back(t):
        def step(f):
            for up, at in enumerate(places):
                s = t - at

                @pl.when((at >= 1) & (at <= s) & (s <= FAR))
                def _():
                    zs = source(half, up, s)
                    block = r_buf.at[half, up, zs, f]
                    back(half, up, s, f, block).wait_recv()

                    @pl.when(at < s)
                    def _():
                        r_buf[half, up, zs, f] = (
                            r_buf[half, up, zs, f].astype(f32) + p_buf[zs, f].astype(f32)
                        ).astype(bf16)
                        hop = jnp.where(at == HALF - 1, s - at, 1)
                        back(half, up, s, f, block, hop).start()

        loop(0, F, step)

    def experts(blocks):
        size = BLOCK * len(blocks)
        gate = jnp.zeros((size, 2 * FFS), f32)
        value = jnp.zeros((size, 2 * FFS), f32)
        for f in range(F):
            cols = slice(f * FW, (f + 1) * FW)
            rows = [x_buf[half, zs, f].reshape(BLOCK, FW) for zs in blocks]
            rows = rows[0] if len(rows) == 1 else jnp.concatenate(rows, axis=0)
            gate, value = [
                total + lax.dot_general(
                    rows, w_in[i, :, :, cols].reshape(2 * FFS, FW),
                    (((1,), (1,)), ((), ())), preferred_element_type=f32,
                )
                for i, total in ((0, gate), (1, value))
            ]
        hidden = (gate / (1.0 + jnp.exp(-gate)) * value).astype(bf16)
        for f in range(F):
            cols = slice(f * FW, (f + 1) * FW)
            part = jnp.dot(
                hidden, w_out[:, :, cols].reshape(2 * FFS, FW), preferred_element_type=f32
            )
            for i, zs in enumerate(blocks):
                p_buf[zs, f] = part[i * BLOCK : (i + 1) * BLOCK].astype(bf16).reshape(
                    NX, 16, FW
                )

    def gathered(f):
        wait_all(a2.at[f, :, pl.ds(0, NX - 1)], x_recv.at[f])
        send_own(f)
        x_buf[half, z, f] = a2[f, half]

    for f in range(F):
        wait_all(a1.at[f, pl.ds(0, NY - 1)], y_recv.at[f])
        b1[f] = jnp.dot(
            by_x, a1[f].reshape(SLOTS, FW), preferred_element_type=f32
        ).astype(bf16).reshape(NX, 2, 16, FW)
        loop(1, NX, lambda k: copy(
            b1.at[f, (x + k) % NX], a2.at[f, :, x], x_send.at[f], x_recv.at[f], x_dev(k)
        ).start())
        a2[f, :, x] = b1[f, x]
        if f:
            gathered(f - 1)
    gathered(F - 1)
    for one in weight_copies:
        one.wait()

    def back_x(o):
        for f in range(F):
            if o == 0:
                total = p_buf[z, f].astype(f32)
                for up, at in enumerate(places):
                    total = total + jnp.where(at >= 1, r_buf[half, up, z, f].astype(f32), 0.0)
                s_buf[o, f] = total.astype(bf16)
            else:
                back(1 - half, near, far, f, r_buf.at[1 - half, near, z, f]).wait_recv()
                s_buf[o, f] = r_buf[1 - half, near, z, f]
            loop(1, NX, lambda k: copy(
                s_buf.at[o, f, (x + k) % NX], t_buf.at[o, f, x],
                xb_send.at[o, f], xb_recv.at[o, f], x_dev(k),
            ).start())
            t_buf[o, f, x] = s_buf[o, f, x]

    def back_y(o):
        for f in range(F):
            wait_all(t_buf.at[o, f, pl.ds(0, NX - 1)], xb_recv.at[o, f])
            rows = t_buf[o, f].reshape(BLOCK, FW)
            total = jnp.dot(by_y[0], rows[:, :FH], preferred_element_type=f32)
            total = total + jnp.dot(by_y[1], rows[:, FH:], preferred_element_type=f32)
            u_buf[o, f] = total.astype(bf16).reshape(NY, 16, FH)
            loop(1, NY, lambda k: copy(
                u_buf.at[o, f, (y + k) % NY], q_buf.at[o, f, y],
                yb_send.at[o, f], yb_recv.at[o, f], y_dev(k),
            ).start())
            q_buf[o, f, y] = u_buf[o, f, y]

    def block_of(up, t):
        at = up * (HALF - 1) + (1 - 2 * up) * u
        return source(half, up, at + t)

    experts([z])
    for t in range(1, FAR + 4):
        if t <= FAR:
            pass_on(t)
        next_back(t)
        if t <= 2:
            experts([block_of(0, t), block_of(1, t)])
        elif t <= 4:
            experts([block_of(near, t)])
        if t == 3:

            @pl.when((u == 1) | (u == 2))
            def _():
                experts([block_of(1 - near, t)])

        if t == 5:

            @pl.when((u == 0) | (u == 3))
            def _():
                experts([block_of(near, t)])

        if t <= FAR:
            first_back(t)
        if t == 6:
            back_x(0)
        if t == 7:
            back_y(0)
    back_x(1)
    back_y(1)

    loop(0, F, lambda f: go(1 - half, near, far, f, a2.at[f, 0]).wait_send())
    for up, at in enumerate(places):
        for s in range(1, FAR + 1):

            @pl.when((at >= 1) & (at <= s))
            def _():
                loop(0, F, lambda f: go(half, up, s, f, a2.at[f, 0]).wait_send())

            @pl.when(at < s)
            def _():
                loop(0, F, lambda f: back(half, up, s, f, p_buf.at[0, f]).wait_send())

    for f in range(F):
        wait_all(o_buf.at[f, pl.ds(0, NY - 1)], y_send.at[f])
        wait_all(a2.at[f, :, pl.ds(0, NX - 1)], x_send.at[f])
        for o in range(2):
            wait_all(t_buf.at[o, f, pl.ds(0, NX - 1)], xb_send.at[o, f])
        wait_all(q_buf.at[0, f, pl.ds(0, NY - 1)], yb_recv.at[0, f])
        wait_all(q_buf.at[1, f, pl.ds(0, NY - 1)], yb_recv.at[1, f])
        for part in range(2):
            cols = slice(f * FW + part * FH, f * FW + (part + 1) * FH)
            moe = jnp.zeros((TOK, FH), f32)
            for o in range(2):
                moe = moe + lax.dot_general(
                    weighting[o][part], q_buf[o, f].reshape(SLOTS, FH),
                    (((0,), (0,)), ((), ())), preferred_element_type=f32,
                )
            mixed = conv[:, cols] + moe / weight_sum
            for i in range(CB):
                out[i, :, cols] = mixed[i * TB : (i + 1) * TB].astype(bf16)
    for f in range(F):
        for o in range(2):
            wait_all(u_buf.at[o, f, pl.ds(0, NY - 1)], yb_send.at[o, f])


def body(tokens, taps, gain, routes, gate_num, gate_proj, up_proj, down_proj):
    anywhere = pl.BlockSpec(memory_space=pl.ANY)
    vmem = pltpu.VMEM
    dma = pltpu.SemaphoreType.DMA
    return pl.pallas_call(
        kernel,
        out_shape=jax.ShapeDtypeStruct((CB, TB, D), bf16),
        in_specs=[anywhere] * 8,
        out_specs=pl.BlockSpec(memory_space=pltpu.VMEM),
        scratch_shapes=[
            vmem((CB, TB, D), bf16),
            vmem((3, 3, D), f32),
            vmem((1, D), f32),
            vmem((2, TOK), jnp.int32),
            vmem((2, TOK), jnp.int32),
            vmem((2, 2, FFS, D), bf16),
            vmem((2, FFS, D), bf16),
            vmem((2, TB, D), f32),
            vmem((2, TB, D), f32),
            vmem((2, TB, D), f32),
            vmem((2, TB, D), f32),
            vmem((2, 2, 1, D), f32),
            vmem((2, 2, 1, D), f32),
            vmem((CB + 2, TB, D), f32),
            vmem((TOK, D), f32),
            vmem((F, NY, 16, FW), bf16),
            vmem((F, NY, 16, FW), bf16),
            vmem((F, NX, 2, 16, FW), bf16),
            vmem((F, 2, NX, 16, FW), bf16),
            vmem((2, NZ, F, NX, 16, FW), bf16),
            vmem((NZ, F, NX, 16, FW), bf16),
            vmem((2, 2, NZ, F, NX, 16, FW), bf16),
            vmem((2, F, NX, 16, FW), bf16),
            vmem((2, F, NX, 16, FW), bf16),
            vmem((2, F, NY, 16, FH), bf16),
            vmem((2, F, NY, 16, FH), bf16),
            dma((8,)),
            dma((3,)),
            dma((3,)),
            dma((8,)),
            dma((8,)),
            dma((F,)),
            dma((F,)),
            dma((F,)),
            dma((F,)),
            dma((4, FAR, F)),
            dma((4, FAR, F)),
            dma((4, FAR, F)),
            dma((4, FAR, F)),
            dma((2, F)),
            dma((2, F)),
            dma((2, F)),
            dma((2, F)),
        ],
        compiler_params=pltpu.CompilerParams(
            collective_id=0, has_side_effects=True, vmem_limit_bytes=56 * 2**20
        ),
    )(
        tokens, taps, gain.reshape(1, D), routes.T, gate_num.T, gate_proj, up_proj, down_proj
    )


def solution(mesh):
    return jax.shard_map(
        body,
        mesh=mesh,
        in_specs=(
            P("chan", "exp", None),
            P(),
            P(),
            P(("chan", "exp"), None),
            P(("chan", "exp"), None),
            P(("exp", "chan"), None, None),
            P(("exp", "chan"), None, None),
            P(("exp", "chan"), None, None),
        ),
        out_specs=P("chan", "exp", None),
        check_vma=False,
    )
```

```python
import jax
import jax.numpy as jnp
from jax import lax
from jax.experimental import pallas as pl
from jax.experimental.pallas import tpu as pltpu
from jax.sharding import PartitionSpec as P

D = 2048
FFS = 176
CB = 6
TB = 8
TOK = CB * TB
NX, NY, NZ = 4, 8, 8
HALF = NZ // 2
CAP = 2
SLOTS = 2 * NX * NY * CAP
BLOCK = NX * NY * CAP
F = 4
FW = D // F
FH = FW // 2
FAR = 5
EPS = 1e-06
MESH = pl.DeviceIdType.MESH
f32 = jnp.float32
bf16 = jnp.bfloat16


def iota(shape, dim):
    return lax.broadcasted_iota(jnp.int32, shape, dim)


def loop(low, high, step):
    def one(k, carry):
        step(k)
        return carry

    lax.fori_loop(low, high, one, 0)


def spread(count, step):
    for k in sorted(range(1, count), key=lambda k: (-min(k, count - k), k)):
        step(k)


def kernel(
    tok_in, taps_in, gain_in, routes_in, numer_in, wg_in, wu_in, wd_in, out,
    tok, taps, gain, routes, numer, w_in, w_out,
    row_send, row_halo, col_send, col_halo, end_send, end_halo, img, conv,
    o_buf, a1, b1, a2, x_buf, p_buf, r_buf, s_buf, t_buf, u_buf, q_buf,
    in_sem, w_send, w_recv, h_send, h_recv, y_send, y_recv, x_send, x_recv,
    go_send, go_recv, back_send, back_recv, xb_send, xb_recv, yb_send, yb_recv,
):
    c = lax.axis_index("chan")
    e = lax.axis_index("exp")
    n_chan = 2 * NZ
    n_exp = NX * NY
    z, core = c // 2, c % 2
    x, y = e // NY, e % NY
    half = z // HALF

    def y_dev(k):
        return (c, x * NY + (y + k) % NY)

    def x_dev(k):
        return (c, ((x + k) % NX) * NY + y)

    def z_dev(k):
        return (((z + k + NZ) % NZ) * 2 + core, e)

    c_low, c_high = (c + n_chan - 1) % n_chan, (c + 1) % n_chan
    e_low, e_high = (e + n_exp - 1) % n_exp, (e + 1) % n_exp

    barrier = pltpu.get_barrier_semaphore()

    def greet(device):
        pl.semaphore_signal(barrier, inc=1, device_id=device, device_id_type=MESH)

    for device in (
        (c_low, e), (c_high, e), (c, e_low), (c, e_high),
        z_dev(1), z_dev(-1), z_dev(2), z_dev(-2),
        (c_low, e_low), (c_low, e_high), (c_high, e_low), (c_high, e_high),
    ):
        greet(device)
    loop(1, NY, lambda k: greet(y_dev(k)))
    loop(1, NX, lambda k: greet(x_dev(k)))

    local = [
        pltpu.make_async_copy(src, dst, in_sem.at[i])
        for i, (src, dst) in enumerate((
            (tok_in, tok), (taps_in, taps), (routes_in, routes), (numer_in, numer),
            (gain_in, gain), (wg_in.at[0], w_in.at[0, 0]), (wu_in.at[0], w_in.at[1, 0]),
            (wd_in.at[0], w_out.at[0]),
        ))
    ]
    for one in local:
        one.start()

    for side in range(2):
        for i in (0, CB + 1):
            col_send[side, i : i + 1] = jnp.zeros((1, D), f32)
    local[0].wait()
    for i in range(CB):
        block = tok[i].astype(f32)
        img[i + 1] = block
        for side, j in enumerate((0, TB - 1)):
            col_send[side, i + 1 : i + 2] = block[j : j + 1]
        for end in range(2):
            if i == end * (CB - 1):
                row_send[end] = block
                for side, j in enumerate((0, TB - 1)):
                    end_send[end, side] = block[j : j + 1]
    pl.semaphore_wait(barrier, 12 + NY - 1 + NX - 1)

    def copy(src, dst, s, r, device):
        return pltpu.make_async_remote_copy(
            src_ref=src, dst_ref=dst, send_sem=s, recv_sem=r, device_id=device, device_id_type=MESH
        )

    c_ends, e_ends = (c_low, c_high), (e_low, e_high)
    halo_copies = []
    for end in range(2):
        for side in range(2):
            i = 4 + 2 * end + side
            halo_copies.append(copy(
                end_send.at[end, side], end_halo.at[1 - end, 1 - side],
                h_send.at[i], h_recv.at[i], (c_ends[end], e_ends[side]),
            ))
    for end in range(2):
        halo_copies.append(copy(
            row_send.at[end], row_halo.at[1 - end], h_send.at[end], h_recv.at[end],
            (c_ends[end], e),
        ))
        halo_copies.append(copy(
            col_send.at[end], col_halo.at[1 - end], h_send.at[2 + end], h_recv.at[2 + end],
            (c, e_ends[end]),
        ))
    for one in halo_copies:
        one.start()
    partner = (z * 2 + 1 - core, e)
    for one in local[5:]:
        one.wait()
    weight_copies = [
        copy(src, dst, w_send.at[i], w_recv.at[i], partner)
        for i, (src, dst) in enumerate((
            (w_in.at[0, 0], w_in.at[0, 1]), (w_in.at[1, 0], w_in.at[1, 1]),
            (w_out.at[0], w_out.at[1]),
        ))
    ]

    for one in local[1:5]:
        one.wait()

    before = (iota((TOK, TOK), 0) < iota((TOK, TOK), 1)).astype(bf16)

    def chosen(expert, cap):
        named = [(routes[q : q + 1] == expert).astype(f32) for q in range(2)]
        earlier = jnp.dot(
            (named[0] + named[1]).astype(bf16), before, preferred_element_type=f32
        )
        in_slot = (earlier == cap.astype(f32)).astype(f32)
        return in_slot * named[0], in_slot * named[1]

    slot = iota((SLOTS, TOK), 0)
    first, second = chosen(
        2 * ((slot // 2 % NX) * NY + slot // 16) + slot // 8 % 2, slot % 2
    )
    placing = (first + second).astype(bf16)
    number = numer[...].astype(f32)
    weighting = []
    for h in (half, 1 - half):
        first, second = chosen(2 * ((slot // 2 % NX) * NY + slot // 16) + h, slot % 2)
        both = first * number[0:1] + second * number[1:2]
        weighting.append([
            (both * (slot // 8 % 2 == part).astype(f32)).astype(bf16) for part in range(2)
        ])
    square = iota((TOK, TOK), 0) == iota((TOK, TOK), 1)
    weight_sum = jnp.sum(
        jnp.where(square, number[0:1] + number[1:2], 0.0), axis=1, keepdims=True
    )

    to = iota((SLOTS, SLOTS), 0)
    by_x = (
        to % 16 // 2 * 16 + to // 16 % 2 * 8 + to // 32 * 2 + to % 2 == iota((SLOTS, SLOTS), 1)
    ).astype(bf16)
    to = iota((SLOTS, BLOCK), 0)
    found = to // 2 % NX * 16 + to // 16 * 2 + to % 2 == iota((SLOTS, BLOCK), 1)
    by_y = [(found & (to // 8 % 2 == part)).astype(bf16) for part in range(2)]

    for one in weight_copies:
        one.start()
    for one in halo_copies:
        one.wait()
    img[0] = jnp.where(c == 0, 0.0, row_halo[0])
    img[CB + 1] = jnp.where(c == n_chan - 1, 0.0, row_halo[1])
    for side in range(2):
        col_halo[side, 0:1] = jnp.where(c == 0, 0.0, end_halo[0, side])
        col_halo[side, CB + 1 : CB + 2] = jnp.where(c == n_chan - 1, 0.0, end_halo[1, side])

    left_end, right_end = e == 0, e == n_exp - 1
    squares = jnp.zeros((TOK, 1), f32)
    place = iota((TB, FW), 0)
    for f in range(F):
        cols = slice(f * FW, (f + 1) * FW)
        rows = []
        for i in range(CB + 2):
            middle = img[i, :, cols]
            low = jnp.where(left_end, 0.0, col_halo[0, i : i + 1, cols])
            high = jnp.where(right_end, 0.0, col_halo[1, i : i + 1, cols])
            rows.append((
                jnp.where(place == 0, low, pltpu.roll(middle, 1, 0)),
                middle,
                jnp.where(place == TB - 1, high, pltpu.roll(middle, TB - 1, 0)),
            ))
        for i in range(CB):
            total = jnp.zeros((TB, FW), f32)
            for a in range(3):
                for b in range(3):
                    total = total + taps[a, b : b + 1, cols] * rows[i + a][b]
            conv[i * TB : (i + 1) * TB, cols] = total
        block = conv[:, cols]
        squares = squares + jnp.sum(block * block, axis=1, keepdims=True)
    inverse = lax.rsqrt(squares * (1.0 / D) + EPS)

    def wait_all(ref, sem):
        pltpu.make_async_copy(ref, ref, sem).wait()

    for f in range(F):
        cols = slice(f * FW, (f + 1) * FW)
        normed = (conv[:, cols] * inverse * gain[:, cols]).astype(bf16)
        o_buf[f] = jnp.dot(placing, normed, preferred_element_type=f32).astype(
            bf16
        ).reshape(NY, 16, FW)
        spread(NY, lambda k: copy(
            o_buf.at[f, (y + k) % NY], a1.at[f, y], y_send.at[f], y_recv.at[f], y_dev(k)
        ).start())
        a1[f, y] = o_buf[f, y]

    u = z % HALF
    places = (u, HALF - 1 - u)
    near = u // 2
    far = HALF + u + near * (HALF - 1 - 2 * u)

    def source(h, up, s):
        return ((1 - 2 * up) * s + 3 * up + HALF * h + NZ) % NZ

    def go(h, up, s, f, src, hop=1):
        way, zs = 2 * h + up, source(h, up, s)
        return copy(
            src, x_buf.at[h, zs, f], go_send.at[way, s - 1, f], go_recv.at[way, s - 1, f],
            z_dev((2 * up - 1) * hop),
        )

    def back(h, up, s, f, src, hop=1):
        way, zs = 2 * h + up, source(h, up, s)
        return copy(
            src, r_buf.at[h, up, zs, f], back_send.at[way, s - 1, f], back_recv.at[way, s - 1, f],
            z_dev((1 - 2 * up) * hop),
        )

    def send_own(f):
        go(1 - half, near, far, f, a2.at[f, 1 - half], far - HALF + 1).start()
        for up, at in enumerate(places):

            @pl.when(at >= 1)
            def _():
                go(half, up, at, f, a2.at[f, half]).start()

    def pass_on(t):
        def step(f):
            for up, at in enumerate(places):
                s = at + t

                @pl.when(s <= FAR)
                def _():
                    block = x_buf.at[half, source(half, up, s), f]
                    go(half, up, s, f, block).wait_recv()

                    @pl.when(at >= 1)
                    def _():
                        go(half, up, s, f, block).start()

        loop(0, F, step)

    def first_back(s):
        for up, at in enumerate(places):

            @pl.when(at == 0)
            def _():
                zs = source(half, up, s)
                loop(0, F, lambda f: back(half, up, s, f, p_buf.at[zs, f]).start())

    def next_back(t):
        def step(f):
            for up, at in enumerate(places):
                s = t - at

                @pl.when((at >= 1) & (at <= s) & (s <= FAR))
                def _():
                    zs = source(half, up, s)
                    block = r_buf.at[half, up, zs, f]
                    back(half, up, s, f, block).wait_recv()

                    @pl.when(at < s)
                    def _():
                        r_buf[half, up, zs, f] = (
                            r_buf[half, up, zs, f].astype(f32) + p_buf[zs, f].astype(f32)
                        ).astype(bf16)
                        hop = jnp.where(at == HALF - 1, s - at, 1)
                        back(half, up, s, f, block, hop).start()

        loop(0, F, step)

    def experts(blocks):
        size = BLOCK * len(blocks)
        gate = jnp.zeros((size, 2 * FFS), f32)
        value = jnp.zeros((size, 2 * FFS), f32)
        for f in range(F):
            cols = slice(f * FW, (f + 1) * FW)
            rows = [x_buf[half, zs, f].reshape(BLOCK, FW) for zs in blocks]
            rows = rows[0] if len(rows) == 1 else jnp.concatenate(rows, axis=0)
            gate, value = [
                total + lax.dot_general(
                    rows, w_in[i, :, :, cols].reshape(2 * FFS, FW),
                    (((1,), (1,)), ((), ())), preferred_element_type=f32,
                )
                for i, total in ((0, gate), (1, value))
            ]
        hidden = (gate / (1.0 + jnp.exp(-gate)) * value).astype(bf16)
        for f in range(F):
            cols = slice(f * FW, (f + 1) * FW)
            part = jnp.dot(
                hidden, w_out[:, :, cols].reshape(2 * FFS, FW), preferred_element_type=f32
            )
            for i, zs in enumerate(blocks):
                p_buf[zs, f] = part[i * BLOCK : (i + 1) * BLOCK].astype(bf16).reshape(
                    NX, 16, FW
                )

    def gathered(f):
        wait_all(a2.at[f, :, pl.ds(0, NX - 1)], x_recv.at[f])
        send_own(f)
        x_buf[half, z, f] = a2[f, half]

    for f in range(F):
        wait_all(a1.at[f, pl.ds(0, NY - 1)], y_recv.at[f])
        b1[f] = jnp.dot(
            by_x, a1[f].reshape(SLOTS, FW), preferred_element_type=f32
        ).astype(bf16).reshape(NX, 2, 16, FW)
        spread(NX, lambda k: copy(
            b1.at[f, (x + k) % NX], a2.at[f, :, x], x_send.at[f], x_recv.at[f], x_dev(k)
        ).start())
        a2[f, :, x] = b1[f, x]
        if f:
            gathered(f - 1)
    gathered(F - 1)
    for one in weight_copies:
        one.wait()

    def back_x(o):
        for f in range(F):
            if o == 0:
                total = p_buf[z, f].astype(f32)
                for up, at in enumerate(places):
                    total = total + jnp.where(at >= 1, r_buf[half, up, z, f].astype(f32), 0.0)
                s_buf[o, f] = total.astype(bf16)
            else:
                back(1 - half, near, far, f, r_buf.at[1 - half, near, z, f]).wait_recv()
                s_buf[o, f] = r_buf[1 - half, near, z, f]
            spread(NX, lambda k: copy(
                s_buf.at[o, f, (x + k) % NX], t_buf.at[o, f, x],
                xb_send.at[o, f], xb_recv.at[o, f], x_dev(k),
            ).start())
            t_buf[o, f, x] = s_buf[o, f, x]

    def back_y(o):
        for f in range(F):
            wait_all(t_buf.at[o, f, pl.ds(0, NX - 1)], xb_recv.at[o, f])
            rows = t_buf[o, f].reshape(BLOCK, FW)
            total = jnp.dot(by_y[0], rows[:, :FH], preferred_element_type=f32)
            total = total + jnp.dot(by_y[1], rows[:, FH:], preferred_element_type=f32)
            u_buf[o, f] = total.astype(bf16).reshape(NY, 16, FH)
            spread(NY, lambda k: copy(
                u_buf.at[o, f, (y + k) % NY], q_buf.at[o, f, y],
                yb_send.at[o, f], yb_recv.at[o, f], y_dev(k),
            ).start())
            q_buf[o, f, y] = u_buf[o, f, y]

    def block_of(up, t):
        at = up * (HALF - 1) + (1 - 2 * up) * u
        return source(half, up, at + t)

    experts([z])
    for t in range(1, FAR + 4):
        if t <= FAR:
            pass_on(t)
        if t <= 2:
            experts([block_of(0, t), block_of(1, t)])
        elif t <= 4:
            experts([block_of(near, t)])
        if t == 3:

            @pl.when((u == 1) | (u == 2))
            def _():
                experts([block_of(1 - near, t)])

        if t == 5:

            @pl.when((u == 0) | (u == 3))
            def _():
                experts([block_of(near, t)])

        if t <= FAR:
            first_back(t)
        next_back(t)
        if t == 6:
            back_x(0)
        if t == 7:
            back_y(0)
    back_x(1)
    back_y(1)

    loop(0, F, lambda f: go(1 - half, near, far, f, a2.at[f, 0]).wait_send())
    for up, at in enumerate(places):
        for s in range(1, FAR + 1):

            @pl.when((at >= 1) & (at <= s))
            def _():
                loop(0, F, lambda f: go(half, up, s, f, a2.at[f, 0]).wait_send())

            @pl.when(at < s)
            def _():
                loop(0, F, lambda f: back(half, up, s, f, p_buf.at[0, f]).wait_send())

    for f in range(F):
        wait_all(o_buf.at[f, pl.ds(0, NY - 1)], y_send.at[f])
        wait_all(a2.at[f, :, pl.ds(0, NX - 1)], x_send.at[f])
        for o in range(2):
            wait_all(t_buf.at[o, f, pl.ds(0, NX - 1)], xb_send.at[o, f])
        wait_all(q_buf.at[0, f, pl.ds(0, NY - 1)], yb_recv.at[0, f])
        wait_all(q_buf.at[1, f, pl.ds(0, NY - 1)], yb_recv.at[1, f])
        for part in range(2):
            cols = slice(f * FW + part * FH, f * FW + (part + 1) * FH)
            moe = jnp.zeros((TOK, FH), f32)
            for o in range(2):
                moe = moe + lax.dot_general(
                    weighting[o][part], q_buf[o, f].reshape(SLOTS, FH),
                    (((0,), (0,)), ((), ())), preferred_element_type=f32,
                )
            mixed = conv[:, cols] + moe / weight_sum
            for i in range(CB):
                out[i, :, cols] = mixed[i * TB : (i + 1) * TB].astype(bf16)
    for f in range(F):
        for o in range(2):
            wait_all(u_buf.at[o, f, pl.ds(0, NY - 1)], yb_send.at[o, f])


def body(tokens, taps, gain, routes, gate_num, gate_proj, up_proj, down_proj):
    anywhere = pl.BlockSpec(memory_space=pl.ANY)
    vmem = pltpu.VMEM
    dma = pltpu.SemaphoreType.DMA
    return pl.pallas_call(
        kernel,
        out_shape=jax.ShapeDtypeStruct((CB, TB, D), bf16),
        in_specs=[anywhere] * 8,
        out_specs=pl.BlockSpec(memory_space=pltpu.VMEM),
        scratch_shapes=[
            vmem((CB, TB, D), bf16),
            vmem((3, 3, D), f32),
            vmem((1, D), f32),
            vmem((2, TOK), jnp.int32),
            vmem((2, TOK), jnp.int32),
            vmem((2, 2, FFS, D), bf16),
            vmem((2, FFS, D), bf16),
            vmem((2, TB, D), f32),
            vmem((2, TB, D), f32),
            vmem((2, TB, D), f32),
            vmem((2, TB, D), f32),
            vmem((2, 2, 1, D), f32),
            vmem((2, 2, 1, D), f32),
            vmem((CB + 2, TB, D), f32),
            vmem((TOK, D), f32),
            vmem((F, NY, 16, FW), bf16),
            vmem((F, NY, 16, FW), bf16),
            vmem((F, NX, 2, 16, FW), bf16),
            vmem((F, 2, NX, 16, FW), bf16),
            vmem((2, NZ, F, NX, 16, FW), bf16),
            vmem((NZ, F, NX, 16, FW), bf16),
            vmem((2, 2, NZ, F, NX, 16, FW), bf16),
            vmem((2, F, NX, 16, FW), bf16),
            vmem((2, F, NX, 16, FW), bf16),
            vmem((2, F, NY, 16, FH), bf16),
            vmem((2, F, NY, 16, FH), bf16),
            dma((8,)),
            dma((3,)),
            dma((3,)),
            dma((8,)),
            dma((8,)),
            dma((F,)),
            dma((F,)),
            dma((F,)),
            dma((F,)),
            dma((4, FAR, F)),
            dma((4, FAR, F)),
            dma((4, FAR, F)),
            dma((4, FAR, F)),
            dma((2, F)),
            dma((2, F)),
            dma((2, F)),
            dma((2, F)),
        ],
        compiler_params=pltpu.CompilerParams(
            collective_id=0, has_side_effects=True, vmem_limit_bytes=56 * 2**20
        ),
    )(
        tokens, taps, gain.reshape(1, D), routes.T, gate_num.T, gate_proj, up_proj, down_proj
    )


def solution(mesh):
    return jax.shard_map(
        body,
        mesh=mesh,
        in_specs=(
            P("chan", "exp", None),
            P(),
            P(),
            P(("chan", "exp"), None),
            P(("chan", "exp"), None),
            P(("exp", "chan"), None, None),
            P(("exp", "chan"), None, None),
            P(("exp", "chan"), None, None),
        ),
        out_specs=P("chan", "exp", None),
        check_vma=False,
    )
```

```python
import jax
import jax.numpy as jnp
from jax import lax
from jax.experimental import pallas as pl
from jax.experimental.pallas import tpu as pltpu
from jax.sharding import PartitionSpec as P

D = 2048
FFS = 176
CB = 6
TB = 8
TOK = CB * TB
NX, NY, NZ = 4, 8, 8
HALF = NZ // 2
CAP = 2
SLOTS = 2 * NX * NY * CAP
BLOCK = NX * NY * CAP
F = 4
FW = D // F
FH = FW // 2
FAR = 5
EPS = 1e-06
MESH = pl.DeviceIdType.MESH
f32 = jnp.float32
bf16 = jnp.bfloat16


def iota(shape, dim):
    return lax.broadcasted_iota(jnp.int32, shape, dim)


def loop(low, high, step):
    def one(k, carry):
        step(k)
        return carry

    lax.fori_loop(low, high, one, 0)


def spread(count, step):
    for k in sorted(range(1, count), key=lambda k: (-min(k, count - k), k)):
        step(k)


def kernel(
    tok_in, taps_in, gain_in, routes_in, numer_in, wg_in, wu_in, wd_in, out,
    tok, taps, gain, routes, numer, w_in, w_out,
    row_send, row_halo, col_send, col_halo, end_send, end_halo, img, conv,
    o_buf, a1, b1, a2, x_buf, p_buf, r_buf, s_buf, t_buf, u_buf, q_buf,
    in_sem, w_send, w_recv, h_send, h_recv, y_send, y_recv, x_send, x_recv,
    go_send, go_recv, back_send, back_recv, xb_send, xb_recv, yb_send, yb_recv,
):
    c = lax.axis_index("chan")
    e = lax.axis_index("exp")
    n_chan = 2 * NZ
    n_exp = NX * NY
    z, core = c // 2, c % 2
    x, y = e // NY, e % NY
    half = z // HALF

    def y_dev(k):
        return (c, x * NY + (y + k) % NY)

    def x_dev(k):
        return (c, ((x + k) % NX) * NY + y)

    def z_dev(k):
        return (((z + k + NZ) % NZ) * 2 + core, e)

    c_low, c_high = (c + n_chan - 1) % n_chan, (c + 1) % n_chan
    e_low, e_high = (e + n_exp - 1) % n_exp, (e + 1) % n_exp

    barrier = pltpu.get_barrier_semaphore()

    def greet(device):
        pl.semaphore_signal(barrier, inc=1, device_id=device, device_id_type=MESH)

    for device in (
        (c_low, e), (c_high, e), (c, e_low), (c, e_high),
        z_dev(1), z_dev(-1), z_dev(2), z_dev(-2),
        (c_low, e_low), (c_low, e_high), (c_high, e_low), (c_high, e_high),
    ):
        greet(device)
    loop(1, NY, lambda k: greet(y_dev(k)))
    loop(1, NX, lambda k: greet(x_dev(k)))

    local = [
        pltpu.make_async_copy(src, dst, in_sem.at[i])
        for i, (src, dst) in enumerate((
            (tok_in, tok), (taps_in, taps), (routes_in, routes), (numer_in, numer),
            (gain_in, gain), (wg_in.at[0], w_in.at[0, 0]), (wu_in.at[0], w_in.at[1, 0]),
            (wd_in.at[0], w_out.at[0]),
        ))
    ]
    for one in local[:5]:
        one.start()

    for side in range(2):
        for i in (0, CB + 1):
            col_send[side, i : i + 1] = jnp.zeros((1, D), f32)
    local[0].wait()
    for i in range(CB):
        block = tok[i].astype(f32)
        img[i + 1] = block
        for side, j in enumerate((0, TB - 1)):
            col_send[side, i + 1 : i + 2] = block[j : j + 1]
        for end in range(2):
            if i == end * (CB - 1):
                row_send[end] = block
                for side, j in enumerate((0, TB - 1)):
                    end_send[end, side] = block[j : j + 1]
    pl.semaphore_wait(barrier, 12 + NY - 1 + NX - 1)

    def copy(src, dst, s, r, device):
        return pltpu.make_async_remote_copy(
            src_ref=src, dst_ref=dst, send_sem=s, recv_sem=r, device_id=device, device_id_type=MESH
        )

    c_ends, e_ends = (c_low, c_high), (e_low, e_high)
    halo_copies = []
    for end in range(2):
        for side in range(2):
            i = 4 + 2 * end + side
            halo_copies.append(copy(
                end_send.at[end, side], end_halo.at[1 - end, 1 - side],
                h_send.at[i], h_recv.at[i], (c_ends[end], e_ends[side]),
            ))
    for end in range(2):
        halo_copies.append(copy(
            row_send.at[end], row_halo.at[1 - end], h_send.at[end], h_recv.at[end],
            (c_ends[end], e),
        ))
        halo_copies.append(copy(
            col_send.at[end], col_halo.at[1 - end], h_send.at[2 + end], h_recv.at[2 + end],
            (c, e_ends[end]),
        ))
    for one in halo_copies:
        one.start()
    for one in local[5:]:
        one.start()
    partner = (z * 2 + 1 - core, e)
    weight_copies = [
        copy(src, dst, w_send.at[i], w_recv.at[i], partner)
        for i, (src, dst) in enumerate((
            (w_in.at[0, 0], w_in.at[0, 1]), (w_in.at[1, 0], w_in.at[1, 1]),
            (w_out.at[0], w_out.at[1]),
        ))
    ]

    for one in local[1:5]:
        one.wait()

    before = (iota((TOK, TOK), 0) < iota((TOK, TOK), 1)).astype(bf16)

    def chosen(expert, cap):
        named = [(routes[q : q + 1] == expert).astype(f32) for q in range(2)]
        earlier = jnp.dot(
            (named[0] + named[1]).astype(bf16), before, preferred_element_type=f32
        )
        in_slot = (earlier == cap.astype(f32)).astype(f32)
        return in_slot * named[0], in_slot * named[1]

    slot = iota((SLOTS, TOK), 0)
    first, second = chosen(
        2 * ((slot // 2 % NX) * NY + slot // 16) + slot // 8 % 2, slot % 2
    )
    placing = (first + second).astype(bf16)
    number = numer[...].astype(f32)
    weighting = []
    for h in (half, 1 - half):
        first, second = chosen(2 * ((slot // 2 % NX) * NY + slot // 16) + h, slot % 2)
        both = first * number[0:1] + second * number[1:2]
        weighting.append([
            (both * (slot // 8 % 2 == part).astype(f32)).astype(bf16) for part in range(2)
        ])
    square = iota((TOK, TOK), 0) == iota((TOK, TOK), 1)
    weight_sum = jnp.sum(
        jnp.where(square, number[0:1] + number[1:2], 0.0), axis=1, keepdims=True
    )

    to = iota((SLOTS, SLOTS), 0)
    by_x = (
        to % 16 // 2 * 16 + to // 16 % 2 * 8 + to // 32 * 2 + to % 2 == iota((SLOTS, SLOTS), 1)
    ).astype(bf16)
    to = iota((SLOTS, BLOCK), 0)
    found = to // 2 % NX * 16 + to // 16 * 2 + to % 2 == iota((SLOTS, BLOCK), 1)
    by_y = [(found & (to // 8 % 2 == part)).astype(bf16) for part in range(2)]

    for one in halo_copies:
        one.wait()
    img[0] = jnp.where(c == 0, 0.0, row_halo[0])
    img[CB + 1] = jnp.where(c == n_chan - 1, 0.0, row_halo[1])
    for side in range(2):
        col_halo[side, 0:1] = jnp.where(c == 0, 0.0, end_halo[0, side])
        col_halo[side, CB + 1 : CB + 2] = jnp.where(c == n_chan - 1, 0.0, end_halo[1, side])

    left_end, right_end = e == 0, e == n_exp - 1
    squares = jnp.zeros((TOK, 1), f32)
    place = iota((TB, FW), 0)
    for f in range(F):
        cols = slice(f * FW, (f + 1) * FW)
        rows = []
        for i in range(CB + 2):
            middle = img[i, :, cols]
            low = jnp.where(left_end, 0.0, col_halo[0, i : i + 1, cols])
            high = jnp.where(right_end, 0.0, col_halo[1, i : i + 1, cols])
            rows.append((
                jnp.where(place == 0, low, pltpu.roll(middle, 1, 0)),
                middle,
                jnp.where(place == TB - 1, high, pltpu.roll(middle, TB - 1, 0)),
            ))
        for i in range(CB):
            total = jnp.zeros((TB, FW), f32)
            for a in range(3):
                for b in range(3):
                    total = total + taps[a, b : b + 1, cols] * rows[i + a][b]
            conv[i * TB : (i + 1) * TB, cols] = total
        block = conv[:, cols]
        squares = squares + jnp.sum(block * block, axis=1, keepdims=True)
    inverse = lax.rsqrt(squares * (1.0 / D) + EPS)

    def wait_all(ref, sem):
        pltpu.make_async_copy(ref, ref, sem).wait()

    for f in range(F):
        cols = slice(f * FW, (f + 1) * FW)
        normed = (conv[:, cols] * inverse * gain[:, cols]).astype(bf16)
        o_buf[f] = jnp.dot(placing, normed, preferred_element_type=f32).astype(
            bf16
        ).reshape(NY, 16, FW)
        spread(NY, lambda k: copy(
            o_buf.at[f, (y + k) % NY], a1.at[f, y], y_send.at[f], y_recv.at[f], y_dev(k)
        ).start())
        a1[f, y] = o_buf[f, y]

    for one in local[5:]:
        one.wait()
    for one in weight_copies:
        one.start()

    u = z % HALF
    places = (u, HALF - 1 - u)
    near = u // 2
    far = HALF + u + near * (HALF - 1 - 2 * u)

    def source(h, up, s):
        return ((1 - 2 * up) * s + 3 * up + HALF * h + NZ) % NZ

    def go(h, up, s, f, src, hop=1):
        way, zs = 2 * h + up, source(h, up, s)
        return copy(
            src, x_buf.at[h, zs, f], go_send.at[way, s - 1, f], go_recv.at[way, s - 1, f],
            z_dev((2 * up - 1) * hop),
        )

    def back(h, up, s, f, src, hop=1):
        way, zs = 2 * h + up, source(h, up, s)
        return copy(
            src, r_buf.at[h, up, zs, f], back_send.at[way, s - 1, f], back_recv.at[way, s - 1, f],
            z_dev((1 - 2 * up) * hop),
        )

    def send_own(f):
        for up, at in enumerate(places):

            @pl.when(at >= 1)
            def _():
                go(half, up, at, f, a2.at[f, half]).start()

        go(1 - half, near, far, f, a2.at[f, 1 - half], far - HALF + 1).start()

    def pass_on(t):
        def step(f):
            for up, at in enumerate(places):
                s = at + t

                @pl.when(s <= FAR)
                def _():
                    block = x_buf.at[half, source(half, up, s), f]
                    go(half, up, s, f, block).wait_recv()

                    @pl.when(at >= 1)
                    def _():
                        go(half, up, s, f, block).start()

        loop(0, F, step)

    def first_back(s):
        for up, at in enumerate(places):

            @pl.when(at == 0)
            def _():
                zs = source(half, up, s)
                loop(0, F, lambda f: back(half, up, s, f, p_buf.at[zs, f]).start())

    def next_back(t):
        def step(f):
            for up, at in enumerate(places):
                s = t - at

                @pl.when((at >= 1) & (at <= s) & (s <= FAR))
                def _():
                    zs = source(half, up, s)
                    block = r_buf.at[half, up, zs, f]
                    back(half, up, s, f, block).wait_recv()

                    @pl.when(at < s)
                    def _():
                        r_buf[half, up, zs, f] = (
                            r_buf[half, up, zs, f].astype(f32) + p_buf[zs, f].astype(f32)
                        ).astype(bf16)
                        hop = jnp.where(at == HALF - 1, s - at, 1)
                        back(half, up, s, f, block, hop).start()

        loop(0, F, step)

    def experts(blocks):
        size = BLOCK * len(blocks)
        gate = jnp.zeros((size, 2 * FFS), f32)
        value = jnp.zeros((size, 2 * FFS), f32)
        for f in range(F):
            cols = slice(f * FW, (f + 1) * FW)
            rows = [x_buf[half, zs, f].reshape(BLOCK, FW) for zs in blocks]
            rows = rows[0] if len(rows) == 1 else jnp.concatenate(rows, axis=0)
            gate, value = [
                total + lax.dot_general(
                    rows, w_in[i, :, :, cols].reshape(2 * FFS, FW),
                    (((1,), (1,)), ((), ())), preferred_element_type=f32,
                )
                for i, total in ((0, gate), (1, value))
            ]
        hidden = (gate / (1.0 + jnp.exp(-gate)) * value).astype(bf16)
        for f in range(F):
            cols = slice(f * FW, (f + 1) * FW)
            part = jnp.dot(
                hidden, w_out[:, :, cols].reshape(2 * FFS, FW), preferred_element_type=f32
            )
            for i, zs in enumerate(blocks):
                p_buf[zs, f] = part[i * BLOCK : (i + 1) * BLOCK].astype(bf16).reshape(
                    NX, 16, FW
                )

    def gathered(f):
        wait_all(a2.at[f, :, pl.ds(0, NX - 1)], x_recv.at[f])
        send_own(f)
        x_buf[half, z, f] = a2[f, half]

    for f in range(F):
        wait_all(a1.at[f, pl.ds(0, NY - 1)], y_recv.at[f])
        b1[f] = jnp.dot(
            by_x, a1[f].reshape(SLOTS, FW), preferred_element_type=f32
        ).astype(bf16).reshape(NX, 2, 16, FW)
        spread(NX, lambda k: copy(
            b1.at[f, (x + k) % NX], a2.at[f, :, x], x_send.at[f], x_recv.at[f], x_dev(k)
        ).start())
        a2[f, :, x] = b1[f, x]
        if f:
            gathered(f - 1)
    gathered(F - 1)
    for one in weight_copies:
        one.wait()

    def back_x(o):
        for f in range(F):
            if o == 0:
                total = p_buf[z, f].astype(f32)
                for up, at in enumerate(places):
                    total = total + jnp.where(at >= 1, r_buf[half, up, z, f].astype(f32), 0.0)
                s_buf[o, f] = total.astype(bf16)
            else:
                back(1 - half, near, far, f, r_buf.at[1 - half, near, z, f]).wait_recv()
                s_buf[o, f] = r_buf[1 - half, near, z, f]
            spread(NX, lambda k: copy(
                s_buf.at[o, f, (x + k) % NX], t_buf.at[o, f, x],
                xb_send.at[o, f], xb_recv.at[o, f], x_dev(k),
            ).start())
            t_buf[o, f, x] = s_buf[o, f, x]

    def back_y(o):
        for f in range(F):
            wait_all(t_buf.at[o, f, pl.ds(0, NX - 1)], xb_recv.at[o, f])
            rows = t_buf[o, f].reshape(BLOCK, FW)
            total = jnp.dot(by_y[0], rows[:, :FH], preferred_element_type=f32)
            total = total + jnp.dot(by_y[1], rows[:, FH:], preferred_element_type=f32)
            u_buf[o, f] = total.astype(bf16).reshape(NY, 16, FH)
            spread(NY, lambda k: copy(
                u_buf.at[o, f, (y + k) % NY], q_buf.at[o, f, y],
                yb_send.at[o, f], yb_recv.at[o, f], y_dev(k),
            ).start())
            q_buf[o, f, y] = u_buf[o, f, y]

    def block_of(up, t):
        at = up * (HALF - 1) + (1 - 2 * up) * u
        return source(half, up, at + t)

    ends = (u == 0) | (u == HALF - 1)
    experts([z])
    for t in range(1, FAR + 4):
        if t <= FAR:
            pass_on(t)
        if t <= 2:
            experts([block_of(0, t), block_of(1, t)])
        elif t <= 4:
            experts([block_of(near, t)])
        if t == 3:

            @pl.when((u == 1) | (u == 2))
            def _():
                experts([block_of(1 - near, t)])

        if t == 5:

            @pl.when((u == 0) | (u == 3))
            def _():
                experts([block_of(near, t)])

        if t <= FAR:
            first_back(t)
        next_back(t)
        if t in (4, 6):

            @pl.when(ends == (t == 6))
            def _():
                back_x(0)

        if t in (5, 7):

            @pl.when(ends == (t == 7))
            def _():
                back_y(0)

    back_x(1)
    back_y(1)

    loop(0, F, lambda f: go(1 - half, near, far, f, a2.at[f, 0]).wait_send())
    for up, at in enumerate(places):
        for s in range(1, FAR + 1):

            @pl.when((at >= 1) & (at <= s))
            def _():
                loop(0, F, lambda f: go(half, up, s, f, a2.at[f, 0]).wait_send())

            @pl.when(at < s)
            def _():
                loop(0, F, lambda f: back(half, up, s, f, p_buf.at[0, f]).wait_send())

    for f in range(F):
        wait_all(o_buf.at[f, pl.ds(0, NY - 1)], y_send.at[f])
        wait_all(a2.at[f, :, pl.ds(0, NX - 1)], x_send.at[f])
        for o in range(2):
            wait_all(t_buf.at[o, f, pl.ds(0, NX - 1)], xb_send.at[o, f])
        wait_all(q_buf.at[0, f, pl.ds(0, NY - 1)], yb_recv.at[0, f])
        wait_all(q_buf.at[1, f, pl.ds(0, NY - 1)], yb_recv.at[1, f])
        for part in range(2):
            cols = slice(f * FW + part * FH, f * FW + (part + 1) * FH)
            moe = jnp.zeros((TOK, FH), f32)
            for o in range(2):
                moe = moe + lax.dot_general(
                    weighting[o][part], q_buf[o, f].reshape(SLOTS, FH),
                    (((0,), (0,)), ((), ())), preferred_element_type=f32,
                )
            mixed = conv[:, cols] + moe / weight_sum
            for i in range(CB):
                out[i, :, cols] = mixed[i * TB : (i + 1) * TB].astype(bf16)
    for f in range(F):
        for o in range(2):
            wait_all(u_buf.at[o, f, pl.ds(0, NY - 1)], yb_send.at[o, f])


def body(tokens, taps, gain, routes, gate_num, gate_proj, up_proj, down_proj):
    anywhere = pl.BlockSpec(memory_space=pl.ANY)
    vmem = pltpu.VMEM
    dma = pltpu.SemaphoreType.DMA
    return pl.pallas_call(
        kernel,
        out_shape=jax.ShapeDtypeStruct((CB, TB, D), bf16),
        in_specs=[anywhere] * 8,
        out_specs=pl.BlockSpec(memory_space=pltpu.VMEM),
        scratch_shapes=[
            vmem((CB, TB, D), bf16),
            vmem((3, 3, D), f32),
            vmem((1, D), f32),
            vmem((2, TOK), jnp.int32),
            vmem((2, TOK), jnp.int32),
            vmem((2, 2, FFS, D), bf16),
            vmem((2, FFS, D), bf16),
            vmem((2, TB, D), f32),
            vmem((2, TB, D), f32),
            vmem((2, TB, D), f32),
            vmem((2, TB, D), f32),
            vmem((2, 2, 1, D), f32),
            vmem((2, 2, 1, D), f32),
            vmem((CB + 2, TB, D), f32),
            vmem((TOK, D), f32),
            vmem((F, NY, 16, FW), bf16),
            vmem((F, NY, 16, FW), bf16),
            vmem((F, NX, 2, 16, FW), bf16),
            vmem((F, 2, NX, 16, FW), bf16),
            vmem((2, NZ, F, NX, 16, FW), bf16),
            vmem((NZ, F, NX, 16, FW), bf16),
            vmem((2, 2, NZ, F, NX, 16, FW), bf16),
            vmem((2, F, NX, 16, FW), bf16),
            vmem((2, F, NX, 16, FW), bf16),
            vmem((2, F, NY, 16, FH), bf16),
            vmem((2, F, NY, 16, FH), bf16),
            dma((8,)),
            dma((3,)),
            dma((3,)),
            dma((8,)),
            dma((8,)),
            dma((F,)),
            dma((F,)),
            dma((F,)),
            dma((F,)),
            dma((4, FAR, F)),
            dma((4, FAR, F)),
            dma((4, FAR, F)),
            dma((4, FAR, F)),
            dma((2, F)),
            dma((2, F)),
            dma((2, F)),
            dma((2, F)),
        ],
        compiler_params=pltpu.CompilerParams(
            collective_id=0, has_side_effects=True, vmem_limit_bytes=56 * 2**20
        ),
    )(
        tokens, taps, gain.reshape(1, D), routes.T, gate_num.T, gate_proj, up_proj, down_proj
    )


def solution(mesh):
    return jax.shard_map(
        body,
        mesh=mesh,
        in_specs=(
            P("chan", "exp", None),
            P(),
            P(),
            P(("chan", "exp"), None),
            P(("chan", "exp"), None),
            P(("exp", "chan"), None, None),
            P(("exp", "chan"), None, None),
            P(("exp", "chan"), None, None),
        ),
        out_specs=P("chan", "exp", None),
        check_vma=False,
    )
```
